512 devices in a mesh: gx: 32 (over x_hi, z), gy: 16 (over y, x_lo, core).
Axes of the slice: x: 4 (x_hi: 2, x_lo: 2; x = x_hi * 2 + x_lo), y: 4, z: 16, core: 2. Of those that a mesh axis runs over, the one named last changes fastest.
Arguments:
- features: bfloat16 [32, 256, 6144], P(None, 'gx', 'gy'), may hold values from -6 to 6
- brick_list: int32 [32, 16, 6], P('gx', 'gy'), may hold values from -1 to 5, as said below
- weight_one: bfloat16 [3, 3, 3, 32, 32], replicated, may hold values from -0.21875 to 0.21875
- weight_two: bfloat16 [3, 3, 3, 32, 32], replicated, may hold values from -0.21875 to 0.21875
- cotangent: bfloat16 [32, 256, 6144], P(None, 'gx', 'gy'), may hold values from -6 to 6
Outputs:
- block_out: bfloat16 [32, 256, 6144], P(None, 'gx', 'gy')
- grad_features: bfloat16 [32, 256, 6144], P(None, 'gx', 'gy')
- grad_one: float32 [3, 3, 3, 32, 32], replicated
- grad_two: float32 [3, 3, 3, 32, 32], replicated
The draws below stay inside these ranges and needn't reach their ends.
Inputs may be any that keep to these rules, and one draw needn't show every extreme that they name: `brick_list`: each device's row first names distinct local bricks (0 to 5), then -1 in the unused slots. Some device lists all of its bricks, some device lists only max(1, 1) of them.
All inputs are finite; a program needn't handle non-finite values.
Results may differ from the reference program's by a relative error of at most 0.003.
Values may be sent and summed in bfloat16 or wider, within the bound.
A program may use at most 128 MiB of HBM per device.

```python
import jax
import jax.numpy as jnp
from jax import lax

C = 32
XB = 1
YB = 1
TBZ = 6
NB = 6
NXV = 256
NYV = 128
NZV = 48
N_GX = 32
N_GY = 16


def draw_brick_list(key, part):
    key = jax.random.fold_in(key, 3)
    count_devices = N_GX * N_GY
    perm_keys = jax.random.split(jax.random.fold_in(key, 11), count_devices)
    orders = jax.vmap(lambda single: jax.random.permutation(single, NB))(perm_keys)
    lowest = max(NB // 4, 1)
    first_key, second_key = jax.random.split(jax.random.fold_in(key, 17))
    first_count = jax.random.randint(first_key, (count_devices,), lowest, NB + 1)
    second_count = jax.random.randint(second_key, (count_devices,), lowest, NB + 1)
    counts = jnp.minimum(first_count, second_count)
    counts = counts.at[0].set(NB).at[count_devices - 1].set(lowest)
    slots = jnp.arange(NB, dtype=jnp.int32)[None, :]
    listed = jnp.where(slots < counts[:, None], orders.astype(jnp.int32), -1)
    return listed.reshape(N_GX, N_GY, NB).astype(jnp.int32)


def level_of(rng, shape, cuts, low, high):
    def one(dim, blocks):
        steps = jax.random.uniform(jax.random.fold_in(jax.random.fold_in(rng, 6), dim), (blocks,), jnp.float32, low / len(cuts), high / len(cuts))
        return jnp.repeat(jnp.exp(steps), shape[dim] // blocks).reshape((-1,) + (1,) * (len(shape) - dim - 1))

    level = one(*cuts[0])
    for cut in cuts[1:]:
        level = level * one(*cut)
    return level


def normal_values(rng, dims, width, reach, cuts=(), kind=jnp.bfloat16):
    array = jax.random.normal(rng, dims, jnp.float32) * width
    if len(cuts) > 0:
        array = level_of(rng, dims, cuts, -0.22, 0.18) * array
    return jnp.clip(array, min=-reach, max=reach).astype(kind)


def setup_inputs(seed: int = 0) -> dict:
    arg_keys = jax.random.split(jax.random.key(seed), 6)
    return {
        "features": normal_values(arg_keys[0], (C, NXV, NYV * NZV), 1.0, 6.0, ((1, 32), (2, 16))),
        "brick_list": draw_brick_list(jax.random.fold_in(arg_keys[5], 71), 0),
        "weight_one": normal_values(arg_keys[2], (3, 3, 3, C, C), (27 * C) ** -0.5, 0.21875),
        "weight_two": normal_values(arg_keys[3], (3, 3, 3, C, C), (27 * C) ** -0.5, 0.21875),
        "cotangent": normal_values(arg_keys[4], (C, NXV, NYV * NZV), 1.0, 6.0, ((1, 32), (2, 16))),
    }


def occupancy(brick_list):
    hits = jax.nn.one_hot(brick_list, NB, dtype=jnp.float32).sum(axis=2)
    hits = hits.reshape(N_GX, N_GY, XB, YB, TBZ).transpose(0, 2, 1, 3, 4).reshape(N_GX * XB, N_GY * YB, TBZ)
    for axis_number in range(3):
        hits = jnp.repeat(hits, 8, axis=axis_number)
    return hits

def shifted_sum(field, weight):
    padded = jnp.pad(field, ((0, 0), (1, 1), (1, 1), (1, 1)))
    size_x, size_y, size_z = (field.shape[1], field.shape[2], field.shape[3])
    running = jnp.zeros(field.shape, jnp.float32)
    for shift_x in range(3):
        for shift_y in range(3):
            for shift_z in range(3):
                window = padded[:, shift_x:shift_x + size_x, shift_y:shift_y + size_y, shift_z:shift_z + size_z]
                running = running + jnp.einsum('ixyz,io->oxyz', window, weight[shift_x, shift_y, shift_z].astype(jnp.float32), precision=lax.Precision.HIGHEST)
    return running

def weight_grad(field, delta):
    padded = jnp.pad(field, ((0, 0), (1, 1), (1, 1), (1, 1)))
    size_x, size_y, size_z = (field.shape[1], field.shape[2], field.shape[3])
    planes = []
    for shift_x in range(3):
        rows_y = []
        for shift_y in range(3):
            rows_z = []
            for shift_z in range(3):
                window = padded[:, shift_x:shift_x + size_x, shift_y:shift_y + size_y, shift_z:shift_z + size_z]
                rows_z.append(jnp.einsum('ixyz,oxyz->io', window, delta, precision=lax.Precision.HIGHEST))
            rows_y.append(jnp.stack(rows_z))
        planes.append(jnp.stack(rows_y))
    return jnp.stack(planes)

def flipped(weight):
    return jnp.swapaxes(jnp.flip(weight, (0, 1, 2)), 3, 4)

def reference(features, brick_list, weight_one, weight_two, cotangent):
    features = features.reshape(C, NXV, NYV, NZV)
    cotangent = cotangent.reshape(C, NXV, NYV, NZV)
    occupied = occupancy(brick_list)
    masked_in = (features.astype(jnp.float32) * occupied).astype(jnp.bfloat16)
    pre_one = occupied * shifted_sum(masked_in.astype(jnp.float32), weight_one)
    hidden = jax.nn.silu(pre_one).astype(jnp.bfloat16)
    pre_two = occupied * shifted_sum(hidden.astype(jnp.float32), weight_two)
    block_out = (masked_in.astype(jnp.float32) + pre_two).astype(jnp.bfloat16)
    grad_masked = (cotangent.astype(jnp.float32) * occupied).astype(jnp.bfloat16)
    grad_hidden = shifted_sum(grad_masked.astype(jnp.float32), flipped(weight_two))
    sigma = jax.nn.sigmoid(pre_one)
    delta_one = (occupied * grad_hidden * sigma * (1.0 + pre_one * (1.0 - sigma))).astype(jnp.bfloat16)
    factor = float(NXV * NYV * NZV) ** (-0.5)
    grad_two = weight_grad(hidden.astype(jnp.float32), grad_masked.astype(jnp.float32)) * factor
    grad_one = weight_grad(masked_in.astype(jnp.float32), delta_one.astype(jnp.float32)) * factor
    back = shifted_sum(delta_one.astype(jnp.float32), flipped(weight_one))
    grad_features = (occupied * (cotangent.astype(jnp.float32) + back)).astype(jnp.bfloat16)
    return (block_out.reshape(C, NXV, NYV * NZV), grad_features.reshape(C, NXV, NYV * NZV), grad_one, grad_two)
```

```python
import functools

import jax
import jax.numpy as jnp
from jax import lax
from jax.experimental import pallas as pl
from jax.experimental.pallas import tpu as pltpu
from jax.sharding import PartitionSpec as P

C = 32
SIDE = 8
NZ = 48
BRICKS = 6
LANES = SIDE * C
OWN = SIDE * NZ
ALL = OWN + 2 * NZ
PACKED = 512
X_HI = 2
MESH = pl.DeviceIdType.MESH
F32 = jnp.float32
BF16 = jnp.bfloat16


def dot(a, b, contract=((1,), (0,))):
    return lax.dot_general(a, b, (contract, ((), ())), preferred_element_type=F32)


def rows_mask(zero_at):
    z = lax.broadcasted_iota(jnp.int32, (NZ, LANES), 0)
    return jnp.concatenate([jnp.where(z == zero_at, 0.0, 1.0).astype(F32)] * SIDE, axis=0)


def from_below(value):
    return pltpu.roll(value, 1, 0) * rows_mask(0)


def from_above(value):
    return pltpu.roll(value, OWN - 1, 0) * rows_mask(NZ - 1)


def at(kx, ky, kz):
    return kx * 9 + ky * 3 + kz


def lane_block(shape=(C, 128)):
    return lax.broadcasted_iota(jnp.int32, shape, 1) // C


def widen_weights(w_ref, quad, which):
    lane = lax.broadcasted_iota(jnp.int32, (C, 128), 1)
    row = lax.broadcasted_iota(jnp.int32, (C, 128), 0)
    repeat = jnp.where(lane % C == row, 1.0, 0.0).astype(BF16)
    quad[which] = dot(w_ref[...], repeat).astype(BF16).reshape(27, C, 128)


def build_bands(quad, band, rim_in, rim_out):
    blocks = lane_block()
    masks = [jnp.where(blocks == b, 1.0, 0.0).astype(BF16) for b in range(4)]
    zero = jnp.zeros((C, 128), BF16)

    def step(i, carry):
        w, ky = i // 3, lax.rem(i, 3)
        rim_in[w, ky] = jnp.zeros((128, 3 * LANES), BF16)
        rim_out[w, ky] = jnp.zeros((LANES, 3 * 128), BF16)
        for kz in range(3):
            parts = [quad[w, at(kx, ky, kz)] for kx in range(3)]
            for xi in range(SIDE):
                for tile in range(2):
                    value = None
                    for kx in range(3):
                        xo = xi + 1 - kx - 4 * tile
                        if 0 <= xo < 4:
                            term = parts[kx] * masks[xo]
                            value = term if value is None else value + term
                    lanes = pl.ds(kz * LANES + tile * 128, 128)
                    band[w, ky, pl.ds(xi * C, C), lanes] = zero if value is None else value
            rim_in[w, ky, pl.ds(0, C), pl.ds(kz * LANES, 128)] = parts[0] * masks[0]
            rim_in[w, ky, pl.ds(C, C), pl.ds(kz * LANES + 128, 128)] = parts[2] * masks[3]
            rim_out[w, ky, pl.ds(0, C), pl.ds(kz * 128, 128)] = parts[2] * masks[2]
            rim_out[w, ky, pl.ds(LANES - C, C), pl.ds(kz * 128, 128)] = parts[0] * masks[3]
        return carry

    lax.fori_loop(0, 6, step, 0)


def shifted_rows(cells, rim, field):
    parts = [cells[field, pl.ds(ky * NZ, OWN), :] for ky in range(3)]
    return jnp.concatenate(parts + [rim[pl.ds(ky * NZ, OWN), :] for ky in range(3)], axis=1)


def conv_forward(cells, rim, band, rim_in, w):
    lhs = shifted_rows(cells, rim, 0)
    terms = []
    for kz in range(3):
        lanes = pl.ds(kz * LANES, LANES)
        rhs = jnp.concatenate(
            [band[w, ky, :, lanes] for ky in range(3)]
            + [rim_in[w, ky, :, lanes] for ky in range(3)],
            axis=0,
        )
        terms.append(dot(lhs, rhs))
    return terms[1] + from_below(terms[0]) + from_above(terms[2])


def conv_backward(cells, rim, band, rim_out, w):
    lhs = shifted_rows(cells, rim, 1)
    terms = []
    for kz in range(3):
        back = 2 - kz
        rhs = jnp.concatenate(
            [band[w, 2 - ky, :, pl.ds(back * LANES, LANES)] for ky in range(3)]
            + [rim_out[w, 2 - ky, :, pl.ds(back * 128, 128)] for ky in range(3)],
            axis=1,
        )
        terms.append(dot(lhs, rhs, ((1,), (1,))))
    return terms[1] + from_below(terms[0]) + from_above(terms[2])


def kernel_sums(own, cells, rim, field):
    wide = own.astype(F32)
    turned = {
        -1: from_above(wide).astype(BF16).T,
        0: own.T,
        1: from_below(wide).astype(BF16).T,
    }
    tall = jnp.concatenate([turned[sz] for sz in (-1, 0, 1)], axis=0)
    ends = jnp.concatenate(
        [turned[sz][part] for sz in (-1, 0, 1) for part in (slice(0, C), slice(LANES - C, LANES))],
        axis=0,
    )
    blocks = lane_block()
    sums = {}
    for sy in (-1, 0, 1):
        rows = pl.ds((1 + sy) * NZ, OWN)
        main = dot(tall, cells[field, rows, :])
        edge = dot(ends, rim[rows, :])
        for n, sz in enumerate((-1, 0, 1)):
            for sx in (-1, 0, 1):
                halves = []
                for tile in range(2):
                    value = None
                    for b in range(4):
                        a = 4 * tile + b - sx
                        if 0 <= a < SIDE:
                            top = n * LANES + a * C
                            term = main[top : top + C, tile * 128 : tile * 128 + 128]
                        else:
                            term = jnp.zeros((C, 128), F32)
                        value = term if value is None else jnp.where(blocks >= b, term, value)
                    halves.append(value)
                total = halves[0] + halves[1]
                if sx == -1:
                    total = total + jnp.where(blocks == 2 * field, edge[n * 64 : n * 64 + C], 0.0)
                if sx == 1:
                    total = total + jnp.where(
                        blocks == 2 * field + 1, edge[n * 64 + C : n * 64 + 64], 0.0
                    )
                sums[sx, sy, sz] = total
    return sums


def fold_four(a, b, c, d):
    blocks = lane_block()
    low = blocks < 2
    middle = (blocks == 1) | (blocks == 2)
    even = (blocks == 0) | (blocks == 2)
    ac = jnp.where(low, a, c) + pltpu.roll(jnp.where(low, c, a), 64, 1)
    bd = jnp.where(middle, b, d) + pltpu.roll(jnp.where(middle, d, b), 64, 1)
    return jnp.where(even, ac, bd) + pltpu.roll(jnp.where(even, bd, ac), 96, 1)


def kernel(
    n_gx, n_gy, factor,
    list_ref, f_ref, g_ref, w1_ref, w2_ref,
    block_ref, back_ref, one_ref, two_ref,
    turned_a, cells_a, side_a, corner_a, rim_a,
    turned_b, cells_b, side_b, corner_b, rim_b,
    quad, band, rim_in, rim_out,
    packed, gathered, column, total,
    halo_send_a, halo_recv_a, halo_send_b, halo_recv_b,
    part_send, part_recv, line_send, line_recv, full_send, full_recv,
):
    gx, gy = lax.axis_index("gx"), lax.axis_index("gy")
    n_line = n_gx // X_HI
    n_plane = X_HI * n_gy
    x_hi, line = gx // n_line, lax.rem(gx, n_line)
    rank = x_hi * n_gy + gy
    share = PACKED // n_plane

    def beside(dx, dy):
        return (lax.rem(gx + dx + n_gx, n_gx), lax.rem(gy + dy + n_gy, n_gy))

    def in_plane(other):
        return (other // n_gy * n_line + line, lax.rem(other, n_gy))

    def in_line(other):
        return (x_hi * n_line + other, gy)

    barrier = pltpu.get_barrier_semaphore()
    around = [(dx, dy) for dx in (-1, 0, 1) for dy in (-1, 0, 1) if (dx, dy) != (0, 0)]
    for dx, dy in around:
        pl.semaphore_signal(barrier, inc=1, device_id=beside(dx, dy), device_id_type=MESH)

    def greet_plane(d, carry):
        target = in_plane(lax.rem(rank + d, n_plane))
        pl.semaphore_signal(barrier, inc=1, device_id=target, device_id_type=MESH)
        return carry

    def greet_line(d, carry):
        target = in_line(lax.rem(line + d, n_line))
        pl.semaphore_signal(barrier, inc=1, device_id=target, device_id_type=MESH)
        return carry

    lax.fori_loop(1, n_plane, greet_plane, 0)
    lax.fori_loop(1, n_line, greet_line, 0)

    hits = []
    for brick in range(BRICKS):
        count = jnp.int32(0)
        for slot in range(BRICKS):
            count = count + jnp.where(list_ref[0, 0, slot] == brick, 1, 0)
        hits.append(count.astype(F32))
    occupied = jnp.concatenate(
        [jnp.full((8, LANES), hit, F32) for hit in hits] * SIDE, axis=0
    )
    brick_of = lax.rem(lax.broadcasted_iota(jnp.int32, (8, OWN), 1), NZ) // 8
    across = jnp.zeros((8, OWN), F32)
    for brick in range(BRICKS):
        across = across + jnp.where(brick_of == brick, hits[brick], 0.0)
    across = jnp.concatenate([across] * (LANES // 8), axis=0)

    row = lax.broadcasted_iota(jnp.int32, (LANES, LANES), 0)
    col = lax.broadcasted_iota(jnp.int32, (LANES, LANES), 1)
    order = jnp.where(col == (row % C) * SIDE + row // C, 1.0, 0.0).astype(BF16)
    reorder = jnp.where(row == (col % C) * SIDE + col // C, 1.0, 0.0).astype(BF16)
    for field, ref in enumerate((f_ref, g_ref)):
        value = (dot(order, ref[...]) * across).astype(BF16)
        turned_a[field] = value
        cells_a[field, pl.ds(NZ, OWN), :] = value.T

    pl.semaphore_wait(barrier, len(around) + n_plane - 1 + n_line - 1)

    def exchange(turned, cells, side, corner, send, recv):
        low, high = pl.ds(0, C), pl.ds(LANES - C, C)
        every, head, tail = pl.ds(0, OWN), pl.ds(0, 128), pl.ds(OWN - 128, 128)

        def strip(rows, lanes):
            return turned.at[:, rows, lanes]

        def slab(y):
            return cells.at[:, pl.ds((y + 1) * NZ, NZ), :]

        plan = [
            (slab(SIDE - 1), slab(-1), (0, 1)),
            (slab(0), slab(SIDE), (0, -1)),
            (strip(high, every), side.at[0], (1, 0)),
            (strip(low, every), side.at[1], (-1, 0)),
            (strip(high, tail), corner.at[0], (1, 1)),
            (strip(low, tail), corner.at[1], (-1, 1)),
            (strip(high, head), corner.at[2], (1, -1)),
            (strip(low, head), corner.at[3], (-1, -1)),
        ]
        copies = []
        for n, (src, dst, (dx, dy)) in enumerate(plan):
            copies.append(
                pltpu.make_async_remote_copy(
                    src_ref=src,
                    dst_ref=dst,
                    send_sem=send.at[n],
                    recv_sem=recv.at[n],
                    device_id=beside(dx, dy),
                    device_id_type=MESH,
                )
            )
        for copy in copies:
            copy.start()
        return copies

    def edge(condition):
        return jnp.where(condition, 1.0, 0.0).astype(F32)

    def place_rims(copies, cells, side, corner, rim):
        for copy in copies:
            copy.wait_recv()
        first_y, last_y = edge(gy > 0), edge(gy < n_gy - 1)
        first_x, last_x = edge(gx > 0), edge(gx < n_gx - 1)
        for rows, keep in ((pl.ds(0, NZ), first_y), (pl.ds(ALL - NZ, NZ), last_y)):
            for field in range(2):
                cells[field, rows, :] = (cells[field, rows, :].astype(F32) * keep).astype(BF16)
        odd = lax.rem(lane_block((1, 128)), 2) == 1
        keep_x = jnp.where(odd, last_x, first_x)

        def turn(left, right):
            parts = [left[0], right[0], left[1], right[1]]
            return jnp.concatenate(parts, axis=0).T.astype(F32) * keep_x

        rim[pl.ds(NZ, OWN), :] = turn(side[0], side[1]).astype(BF16)
        upper = turn(corner[0], corner[1])[128 - NZ :] * first_y
        lower = turn(corner[2], corner[3])[:NZ] * last_y
        rim[pl.ds(0, NZ), :] = upper.astype(BF16)
        rim[pl.ds(ALL - NZ, NZ), :] = lower.astype(BF16)

    copies_a = exchange(turned_a, cells_a, side_a, corner_a, halo_send_a, halo_recv_a)
    widen_weights(w1_ref, quad, 0)
    widen_weights(w2_ref, quad, 1)
    build_bands(quad, band, rim_in, rim_out)
    place_rims(copies_a, cells_a, side_a, corner_a, rim_a)

    pre_one = conv_forward(cells_a, rim_a, band, rim_in, 0) * occupied
    sigma = jax.nn.sigmoid(pre_one)
    hidden = (pre_one * sigma).astype(BF16)
    slope = occupied * sigma * (1.0 + pre_one * (1.0 - sigma))
    delta = (conv_backward(cells_a, rim_a, band, rim_out, 1) * slope).astype(BF16)
    for field, value in enumerate((hidden, delta)):
        cells_b[field, pl.ds(NZ, OWN), :] = value
        turned_b[field] = value.T
    copies_b = exchange(turned_b, cells_b, side_b, corner_b, halo_send_b, halo_recv_b)

    sums_two = kernel_sums(hidden, cells_a, rim_a, 1)
    sums_one = kernel_sums(delta, cells_a, rim_a, 0)
    offsets = [(kx, ky, kz) for kx in (-1, 0, 1) for ky in (-1, 0, 1) for kz in (-1, 0, 1)]
    one = [sums_one[k] for k in offsets] + [jnp.zeros((C, 128), F32)]
    two = [sums_two[-k[0], -k[1], -k[2]] for k in offsets] + [jnp.zeros((C, 128), F32)]
    for n, start in enumerate(range(0, 28, 4)):
        packed[pl.ds(n * C, C), :] = fold_four(*one[start : start + 4])
        packed[pl.ds((7 + n) * C, C), :] = fold_four(*two[start : start + 4])
    packed[pl.ds(14 * C, PACKED - 14 * C), :] = jnp.zeros((PACKED - 14 * C, 128), F32)

    def share_of(ref, other):
        return ref.at[pl.ds(pl.multiple_of(other * share, share), share), :]

    def part_copy(target, source):
        return pltpu.make_async_remote_copy(
            src_ref=share_of(packed, target),
            dst_ref=gathered.at[source],
            send_sem=part_send.at[target],
            recv_sem=part_recv.at[source],
            device_id=in_plane(target),
            device_id_type=MESH,
        )

    def line_copy(target, source):
        return pltpu.make_async_remote_copy(
            src_ref=column.at[line],
            dst_ref=column.at[source],
            send_sem=line_send.at[target],
            recv_sem=line_recv.at[source],
            device_id=in_line(target),
            device_id_type=MESH,
        )

    def full_copy(target, source):
        return pltpu.make_async_remote_copy(
            src_ref=share_of(total, rank),
            dst_ref=share_of(total, source),
            send_sem=full_send.at[target],
            recv_sem=full_recv.at[source],
            device_id=in_plane(target),
            device_id_type=MESH,
        )

    def each(make, me, count, act):
        def step(d, carry):
            act(make, me, lax.rem(me + d, count))
            return carry

        lax.fori_loop(1, count, step, 0)

    def start(make, me, other):
        make(other, me).start()

    def landed(make, me, other):
        make(other, other).wait_recv()

    def sent(make, me, other):
        make(other, me).wait_send()

    def summed(ref, count):
        value = ref[0]
        for n in range(1, count):
            value = value + ref[n]
        return value

    each(part_copy, rank, n_plane, start)
    gathered[rank] = packed[pl.ds(pl.multiple_of(rank * share, share), share), :]

    place_rims(copies_b, cells_b, side_b, corner_b, rim_b)
    pre_two = conv_forward(cells_b, rim_b, band, rim_in, 1) * occupied
    middle = pl.ds(NZ, OWN)
    block_out = (cells_a[0, middle, :].astype(F32) + pre_two).astype(BF16)
    block_ref[...] = dot(reorder, block_out, ((1,), (1,))).astype(BF16)

    each(part_copy, rank, n_plane, landed)
    column[line] = summed(gathered, n_plane)
    each(line_copy, line, n_line, start)

    back = conv_backward(cells_b, rim_b, band, rim_out, 0) * occupied
    grad_features = (cells_a[1, middle, :].astype(F32) + back).astype(BF16)
    back_ref[...] = dot(reorder, grad_features, ((1,), (1,))).astype(BF16)

    each(line_copy, line, n_line, landed)
    total[pl.ds(pl.multiple_of(rank * share, share), share), :] = summed(column, n_line)
    each(full_copy, rank, n_plane, start)
    for copy in copies_a + copies_b:
        copy.wait_send()
    each(part_copy, rank, n_plane, sent)
    each(line_copy, line, n_line, sent)
    each(full_copy, rank, n_plane, landed)

    for n, first in enumerate(range(0, 27, 4)):
        count = min(4, 27 - first)
        one_ref[pl.ds(first * C, count * C), :] = (
            total[pl.ds(n * C, C), :].T[: count * C] * factor
        )
        group = total[pl.ds((7 + n) * C, C), :] * factor
        for k in range(count):
            two_ref[pl.ds((first + k) * C, C), :] = group[:, k * C : (k + 1) * C]
    each(full_copy, rank, n_plane, sent)


def per_device(features, brick_list, weight_one, weight_two, cotangent):
    n_gx, n_gy = lax.axis_size("gx"), lax.axis_size("gy")
    n_line, n_plane = n_gx // X_HI, X_HI * n_gy
    share = PACKED // n_plane
    factor = float(n_gx * SIDE * n_gy * SIDE * NZ) ** (-0.5)
    vmem = pl.BlockSpec(memory_space=pltpu.VMEM)
    halo = [
        pltpu.VMEM((2, LANES, OWN), BF16),
        pltpu.VMEM((2, ALL, LANES), BF16),
        pltpu.VMEM((2, 2, C, OWN), BF16),
        pltpu.VMEM((4, 2, C, 128), BF16),
        pltpu.VMEM((ALL, 128), BF16),
    ]
    block_out, grad_features, one, two = pl.pallas_call(
        functools.partial(kernel, n_gx, n_gy, factor),
        out_shape=(
            jax.ShapeDtypeStruct((LANES, OWN), BF16),
            jax.ShapeDtypeStruct((LANES, OWN), BF16),
            jax.ShapeDtypeStruct((27 * C, C), F32),
            jax.ShapeDtypeStruct((27 * C, C), F32),
        ),
        in_specs=[pl.BlockSpec(memory_space=pltpu.SMEM)] + [vmem] * 4,
        out_specs=[vmem] * 4,
        scratch_shapes=halo
        + halo
        + [
            pltpu.VMEM((2, 27, C, 128), BF16),
            pltpu.VMEM((2, 3, LANES, 3 * LANES), BF16),
            pltpu.VMEM((2, 3, 128, 3 * LANES), BF16),
            pltpu.VMEM((2, 3, LANES, 3 * 128), BF16),
            pltpu.VMEM((PACKED, 128), F32),
            pltpu.VMEM((n_plane, share, 128), F32),
            pltpu.VMEM((n_line, share, 128), F32),
            pltpu.VMEM((PACKED, 128), F32),
        ]
        + [pltpu.SemaphoreType.DMA((8,))] * 4
        + [pltpu.SemaphoreType.DMA((n_plane,))] * 2
        + [pltpu.SemaphoreType.DMA((n_line,))] * 2
        + [pltpu.SemaphoreType.DMA((n_plane,))] * 2,
        compiler_params=pltpu.CompilerParams(
            collective_id=0, has_side_effects=True, vmem_limit_bytes=48 * 1024 * 1024
        ),
    )(
        brick_list,
        features.reshape(LANES, OWN),
        cotangent.reshape(LANES, OWN),
        weight_one.reshape(27 * C, C),
        weight_two.reshape(27 * C, C),
    )
    flat = (C, SIDE, OWN)
    cube = (3, 3, 3, C, C)
    return block_out.reshape(flat), grad_features.reshape(flat), one.reshape(cube), two.reshape(cube)


def solution(mesh):
    return jax.shard_map(
        per_device,
        mesh=mesh,
        in_specs=(P(None, "gx", "gy"), P("gx", "gy", None), P(), P(), P(None, "gx", "gy")),
        out_specs=(P(None, "gx", "gy"), P(None, "gx", "gy"), P(), P()),
        check_vma=False,
    )
```

```python
import functools

import jax
import jax.numpy as jnp
from jax import lax
from jax.experimental import pallas as pl
from jax.experimental.pallas import tpu as pltpu
from jax.sharding import PartitionSpec as P

C = 32
SIDE = 8
NZ = 48
BRICKS = 6
LANES = SIDE * C
OWN = SIDE * NZ
ALL = OWN + 2 * NZ
PACKED = 512
X_HI = 2
MESH = pl.DeviceIdType.MESH
F32 = jnp.float32
BF16 = jnp.bfloat16


def dot(a, b, contract=((1,), (0,))):
    return lax.dot_general(a, b, (contract, ((), ())), preferred_element_type=F32)


def rows_mask(zero_at):
    z = lax.broadcasted_iota(jnp.int32, (NZ, LANES), 0)
    return jnp.concatenate([jnp.where(z == zero_at, 0.0, 1.0).astype(F32)] * SIDE, axis=0)


def from_below(value):
    return pltpu.roll(value, 1, 0) * rows_mask(0)


def from_above(value):
    return pltpu.roll(value, OWN - 1, 0) * rows_mask(NZ - 1)


def at(kx, ky, kz):
    return kx * 9 + ky * 3 + kz


def lane_block(shape=(C, 128)):
    return lax.broadcasted_iota(jnp.int32, shape, 1) // C


def widen_weights(w_ref, quad, which):
    lane = lax.broadcasted_iota(jnp.int32, (C, 128), 1)
    row = lax.broadcasted_iota(jnp.int32, (C, 128), 0)
    repeat = jnp.where(lane % C == row, 1.0, 0.0).astype(BF16)
    quad[which] = dot(w_ref[which], repeat).astype(BF16).reshape(27, C, 128)


def build_bands(quad, band, rim_in, rim_out):
    blocks = lane_block()
    masks = [jnp.where(blocks == b, 1.0, 0.0).astype(BF16) for b in range(4)]
    zero = jnp.zeros((C, 128), BF16)

    def step(i, carry):
        w, ky = i // 3, lax.rem(i, 3)
        rim_in[w, ky] = jnp.zeros((128, 3 * LANES), BF16)
        rim_out[w, ky] = jnp.zeros((LANES, 3 * 128), BF16)
        for kz in range(3):
            parts = [quad[w, at(kx, ky, kz)] for kx in range(3)]
            for xi in range(SIDE):
                for tile in range(2):
                    value = None
                    for kx in range(3):
                        xo = xi + 1 - kx - 4 * tile
                        if 0 <= xo < 4:
                            term = parts[kx] * masks[xo]
                            value = term if value is None else value + term
                    lanes = pl.ds(kz * LANES + tile * 128, 128)
                    band[w, ky, pl.ds(xi * C, C), lanes] = zero if value is None else value
            rim_in[w, ky, pl.ds(0, C), pl.ds(kz * LANES, 128)] = parts[0] * masks[0]
            rim_in[w, ky, pl.ds(C, C), pl.ds(kz * LANES + 128, 128)] = parts[2] * masks[3]
            rim_out[w, ky, pl.ds(0, C), pl.ds(kz * 128, 128)] = parts[2] * masks[2]
            rim_out[w, ky, pl.ds(LANES - C, C), pl.ds(kz * 128, 128)] = parts[0] * masks[3]
        return carry

    lax.fori_loop(0, 6, step, 0)


def shifted_rows(cells, rim, field):
    parts = [cells[field, pl.ds(ky * NZ, OWN), :] for ky in range(3)]
    return jnp.concatenate(parts + [rim[pl.ds(ky * NZ, OWN), :] for ky in range(3)], axis=1)


def conv_forward(cells, rim, band, rim_in, w):
    lhs = shifted_rows(cells, rim, 0)
    terms = []
    for kz in range(3):
        lanes = pl.ds(kz * LANES, LANES)
        rhs = jnp.concatenate(
            [band[w, ky, :, lanes] for ky in range(3)]
            + [rim_in[w, ky, :, lanes] for ky in range(3)],
            axis=0,
        )
        terms.append(dot(lhs, rhs))
    return terms[1] + from_below(terms[0]) + from_above(terms[2])


def conv_backward(cells, rim, band, rim_out, w):
    lhs = shifted_rows(cells, rim, 1)
    terms = []
    for kz in range(3):
        back = 2 - kz
        rhs = jnp.concatenate(
            [band[w, 2 - ky, :, pl.ds(back * LANES, LANES)] for ky in range(3)]
            + [rim_out[w, 2 - ky, :, pl.ds(back * 128, 128)] for ky in range(3)],
            axis=1,
        )
        terms.append(dot(lhs, rhs, ((1,), (1,))))
    return terms[1] + from_below(terms[0]) + from_above(terms[2])


def kernel_sums(own, cells, rim, field):
    wide = own.astype(F32)
    turned = {
        -1: from_above(wide).astype(BF16).T,
        0: own.T,
        1: from_below(wide).astype(BF16).T,
    }
    tall = jnp.concatenate([turned[sz] for sz in (-1, 0, 1)], axis=0)
    ends = jnp.concatenate(
        [turned[sz][part] for sz in (-1, 0, 1) for part in (slice(0, C), slice(LANES - C, LANES))],
        axis=0,
    )
    blocks = lane_block()
    sums = {}
    for sy in (-1, 0, 1):
        rows = pl.ds((1 + sy) * NZ, OWN)
        main = dot(tall, cells[field, rows, :])
        edge = dot(ends, rim[rows, :])
        for n, sz in enumerate((-1, 0, 1)):
            for sx in (-1, 0, 1):
                halves = []
                for tile in range(2):
                    value = None
                    for b in range(4):
                        a = 4 * tile + b - sx
                        if 0 <= a < SIDE:
                            top = n * LANES + a * C
                            term = main[top : top + C, tile * 128 : tile * 128 + 128]
                        else:
                            term = jnp.zeros((C, 128), F32)
                        value = term if value is None else jnp.where(blocks >= b, term, value)
                    halves.append(value)
                total = halves[0] + halves[1]
                if sx == -1:
                    total = total + jnp.where(blocks == 2 * field, edge[n * 64 : n * 64 + C], 0.0)
                if sx == 1:
                    total = total + jnp.where(
                        blocks == 2 * field + 1, edge[n * 64 + C : n * 64 + 64], 0.0
                    )
                sums[sx, sy, sz] = total
    return sums


def fold_four(a, b, c, d):
    blocks = lane_block()
    low = blocks < 2
    middle = (blocks == 1) | (blocks == 2)
    even = (blocks == 0) | (blocks == 2)
    ac = jnp.where(low, a, c) + pltpu.roll(jnp.where(low, c, a), 64, 1)
    bd = jnp.where(middle, b, d) + pltpu.roll(jnp.where(middle, d, b), 64, 1)
    return jnp.where(even, ac, bd) + pltpu.roll(jnp.where(even, bd, ac), 96, 1)


def kernel(
    n_gx, n_gy, factor,
    list_any, f_any, g_any, w1_any, w2_any,
    block_ref, back_ref, one_ref, two_ref,
    turned_a, cells_a, side_a, corner_a, rim_a,
    turned_b, cells_b, side_b, corner_b, rim_b,
    quad, band, rim_in, rim_out,
    packed, gathered, column, total,
    list_ref, fields_in, weights_in,
    list_sem, f_sem, g_sem, w1_sem, w2_sem,
    halo_send_a, halo_recv_a, halo_send_b, halo_recv_b,
    part_send, part_recv, line_send, line_recv, full_send, full_recv,
):
    gx, gy = lax.axis_index("gx"), lax.axis_index("gy")
    n_line = n_gx // X_HI
    n_plane = X_HI * n_gy
    x_hi, line = gx // n_line, lax.rem(gx, n_line)
    rank = x_hi * n_gy + gy
    share = PACKED // n_plane

    def beside(dx, dy):
        return (lax.rem(gx + dx + n_gx, n_gx), lax.rem(gy + dy + n_gy, n_gy))

    def in_plane(other):
        return (other // n_gy * n_line + line, lax.rem(other, n_gy))

    def in_line(other):
        return (x_hi * n_line + other, gy)

    loads = [
        pltpu.make_async_copy(src, dst, sem)
        for src, dst, sem in (
            (list_any, list_ref, list_sem),
            (f_any, fields_in.at[0], f_sem),
            (g_any, fields_in.at[1], g_sem),
            (w1_any, weights_in.at[0], w1_sem),
            (w2_any, weights_in.at[1], w2_sem),
        )
    ]
    for load in loads:
        load.start()

    barrier = pltpu.get_barrier_semaphore()
    around = [(dx, dy) for dx in (-1, 0, 1) for dy in (-1, 0, 1) if (dx, dy) != (0, 0)]
    for dx, dy in around:
        pl.semaphore_signal(barrier, inc=1, device_id=beside(dx, dy), device_id_type=MESH)

    def greet_plane(d, carry):
        target = in_plane(lax.rem(rank + d, n_plane))
        pl.semaphore_signal(barrier, inc=1, device_id=target, device_id_type=MESH)
        return carry

    def greet_line(d, carry):
        target = in_line(lax.rem(line + d, n_line))
        pl.semaphore_signal(barrier, inc=1, device_id=target, device_id_type=MESH)
        return carry

    lax.fori_loop(1, n_plane, greet_plane, 0)
    lax.fori_loop(1, n_line, greet_line, 0)

    loads[0].wait()
    hits = []
    for brick in range(BRICKS):
        count = jnp.int32(0)
        for slot in range(BRICKS):
            count = count + jnp.where(list_ref[0, 0, slot] == brick, 1, 0)
        hits.append(count.astype(F32))
    occupied = jnp.concatenate(
        [jnp.full((8, LANES), hit, F32) for hit in hits] * SIDE, axis=0
    )
    brick_of = lax.rem(lax.broadcasted_iota(jnp.int32, (8, OWN), 1), NZ) // 8
    across = jnp.zeros((8, OWN), F32)
    for brick in range(BRICKS):
        across = across + jnp.where(brick_of == brick, hits[brick], 0.0)
    across = jnp.concatenate([across] * (LANES // 8), axis=0)

    row = lax.broadcasted_iota(jnp.int32, (LANES, LANES), 0)
    col = lax.broadcasted_iota(jnp.int32, (LANES, LANES), 1)
    order = jnp.where(col == (row % C) * SIDE + row // C, 1.0, 0.0).astype(BF16)
    reorder = jnp.where(row == (col % C) * SIDE + col // C, 1.0, 0.0).astype(BF16)
    for field in range(2):
        loads[1 + field].wait()
        value = (dot(order, fields_in[field]) * across).astype(BF16)
        turned_a[field] = value
        cells_a[field, pl.ds(NZ, OWN), :] = value.T

    pl.semaphore_wait(barrier, len(around) + n_plane - 1 + n_line - 1)

    def exchange(turned, cells, side, corner, send, recv):
        low, high = pl.ds(0, C), pl.ds(LANES - C, C)
        every, head, tail = pl.ds(0, OWN), pl.ds(0, 128), pl.ds(OWN - 128, 128)

        def strip(rows, lanes):
            return turned.at[:, rows, lanes]

        def slab(y):
            return cells.at[:, pl.ds((y + 1) * NZ, NZ), :]

        plan = [
            (strip(high, tail), corner.at[0], (1, 1)),
            (strip(low, tail), corner.at[1], (-1, 1)),
            (strip(high, head), corner.at[2], (1, -1)),
            (strip(low, head), corner.at[3], (-1, -1)),
            (slab(SIDE - 1), slab(-1), (0, 1)),
            (slab(0), slab(SIDE), (0, -1)),
            (strip(high, every), side.at[0], (1, 0)),
            (strip(low, every), side.at[1], (-1, 0)),
        ]
        copies = []
        for src, dst, (dx, dy) in plan:
            copies.append(
                pltpu.make_async_remote_copy(
                    src_ref=src,
                    dst_ref=dst,
                    send_sem=send,
                    recv_sem=recv,
                    device_id=beside(dx, dy),
                    device_id_type=MESH,
                )
            )
        for copy in copies:
            copy.start()
        whole = turned.at[:, :, pl.ds(0, 256)]
        return pltpu.make_async_remote_copy(
            src_ref=whole,
            dst_ref=whole,
            send_sem=send,
            recv_sem=recv,
            device_id=beside(1, 0),
            device_id_type=MESH,
        )

    def edge(condition):
        return jnp.where(condition, 1.0, 0.0).astype(F32)

    def place_rims(copies, cells, side, corner, rim):
        copies.wait_recv()
        first_y, last_y = edge(gy > 0), edge(gy < n_gy - 1)
        first_x, last_x = edge(gx > 0), edge(gx < n_gx - 1)
        for rows, keep in ((pl.ds(0, NZ), first_y), (pl.ds(ALL - NZ, NZ), last_y)):
            for field in range(2):
                cells[field, rows, :] = (cells[field, rows, :].astype(F32) * keep).astype(BF16)
        odd = lax.rem(lane_block((1, 128)), 2) == 1
        keep_x = jnp.where(odd, last_x, first_x)

        def turn(left, right):
            parts = [left[0], right[0], left[1], right[1]]
            return jnp.concatenate(parts, axis=0).T.astype(F32) * keep_x

        rim[pl.ds(NZ, OWN), :] = turn(side[0], side[1]).astype(BF16)
        upper = turn(corner[0], corner[1])[128 - NZ :] * first_y
        lower = turn(corner[2], corner[3])[:NZ] * last_y
        rim[pl.ds(0, NZ), :] = upper.astype(BF16)
        rim[pl.ds(ALL - NZ, NZ), :] = lower.astype(BF16)

    copies_a = exchange(turned_a, cells_a, side_a, corner_a, halo_send_a, halo_recv_a)
    for w in range(2):
        loads[3 + w].wait()
        widen_weights(weights_in, quad, w)
    build_bands(quad, band, rim_in, rim_out)
    place_rims(copies_a, cells_a, side_a, corner_a, rim_a)

    pre_one = conv_forward(cells_a, rim_a, band, rim_in, 0) * occupied
    sigma = jax.nn.sigmoid(pre_one)
    hidden = (pre_one * sigma).astype(BF16)
    slope = occupied * sigma * (1.0 + pre_one * (1.0 - sigma))
    delta = (conv_backward(cells_a, rim_a, band, rim_out, 1) * slope).astype(BF16)
    for field, value in enumerate((hidden, delta)):
        cells_b[field, pl.ds(NZ, OWN), :] = value
        turned_b[field] = value.T
    copies_b = exchange(turned_b, cells_b, side_b, corner_b, halo_send_b, halo_recv_b)

    sums_two = kernel_sums(hidden, cells_a, rim_a, 1)
    sums_one = kernel_sums(delta, cells_a, rim_a, 0)
    offsets = [(kx, ky, kz) for kx in (-1, 0, 1) for ky in (-1, 0, 1) for kz in (-1, 0, 1)]
    one = [sums_one[k] for k in offsets] + [jnp.zeros((C, 128), F32)]
    two = [sums_two[-k[0], -k[1], -k[2]] for k in offsets] + [jnp.zeros((C, 128), F32)]
    for n, start in enumerate(range(0, 28, 4)):
        packed[pl.ds(n * C, C), :] = fold_four(*one[start : start + 4])
        packed[pl.ds((7 + n) * C, C), :] = fold_four(*two[start : start + 4])
    packed[pl.ds(14 * C, PACKED - 14 * C), :] = jnp.zeros((PACKED - 14 * C, 128), F32)

    def share_of(ref, other):
        return ref.at[pl.ds(pl.multiple_of(other * share, share), share), :]

    def remote(src, dst, send, recv, device):
        return pltpu.make_async_remote_copy(
            src_ref=src,
            dst_ref=dst,
            send_sem=send,
            recv_sem=recv,
            device_id=device,
            device_id_type=MESH,
        )

    def part_copy(target):
        src, dst = share_of(packed, target), gathered.at[rank]
        return remote(src, dst, part_send, part_recv, in_plane(target))

    def line_copy(target):
        src, dst = column.at[line], column.at[line]
        return remote(src, dst, line_send, line_recv, in_line(target))

    def full_copy(target):
        src, dst = share_of(total, rank), share_of(total, rank)
        return remote(src, dst, full_send, full_recv, in_plane(target))

    def start_all(make, me, count):
        def step(d, carry):
            make(lax.rem(me + d, count)).start()
            return carry

        lax.fori_loop(1, count, step, 0)

    most = gathered.at[pl.ds(0, n_plane - 1)]
    part_all = remote(most, most, part_send, part_recv, beside(1, 0))
    most = column.at[pl.ds(0, n_line - 1)]
    line_all = remote(most, most, line_send, line_recv, beside(1, 0))
    most = total.at[pl.ds(0, (n_plane - 1) * share)]
    full_all = remote(most, most, full_send, full_recv, beside(1, 0))

    def summed(ref, count):
        value = ref[0].astype(F32)
        for n in range(1, count):
            value = value + ref[n].astype(F32)
        return value

    start_all(part_copy, rank, n_plane)
    gathered[rank] = packed[pl.ds(pl.multiple_of(rank * share, share), share), :]

    place_rims(copies_b, cells_b, side_b, corner_b, rim_b)
    pre_two = conv_forward(cells_b, rim_b, band, rim_in, 1) * occupied
    middle = pl.ds(NZ, OWN)
    block_out = (cells_a[0, middle, :].astype(F32) + pre_two).astype(BF16)
    block_ref[...] = dot(reorder, block_out, ((1,), (1,))).astype(BF16)

    part_all.wait_recv()
    column[line] = summed(gathered, n_plane).astype(BF16)
    start_all(line_copy, line, n_line)

    back = conv_backward(cells_b, rim_b, band, rim_out, 0) * occupied
    grad_features = (cells_a[1, middle, :].astype(F32) + back).astype(BF16)
    back_ref[...] = dot(reorder, grad_features, ((1,), (1,))).astype(BF16)

    line_all.wait_recv()
    total[pl.ds(pl.multiple_of(rank * share, share), share), :] = summed(column, n_line)
    start_all(full_copy, rank, n_plane)
    for copies in (copies_a, copies_b, part_all, line_all):
        copies.wait_send()
    full_all.wait_recv()

    for n, first in enumerate(range(0, 27, 4)):
        count = min(4, 27 - first)
        one_ref[pl.ds(first * C, count * C), :] = (
            total[pl.ds(n * C, C), :].T[: count * C] * factor
        )
        group = total[pl.ds((7 + n) * C, C), :] * factor
        for k in range(count):
            two_ref[pl.ds((first + k) * C, C), :] = group[:, k * C : (k + 1) * C]
    full_all.wait_send()


def deliver(*refs):
    results, outs, sems = refs[:4], refs[4:8], refs[8:]
    copies = [pltpu.make_async_copy(*part) for part in zip(results, outs, sems)]
    for copy in copies:
        copy.start()
    for copy in copies:
        copy.wait()


def per_device(features, brick_list, weight_one, weight_two, cotangent):
    n_gx, n_gy = lax.axis_size("gx"), lax.axis_size("gy")
    n_line, n_plane = n_gx // X_HI, X_HI * n_gy
    share = PACKED // n_plane
    factor = float(n_gx * SIDE * n_gy * SIDE * NZ) ** (-0.5)
    vmem = pl.BlockSpec(memory_space=pltpu.VMEM)
    halo = [
        pltpu.VMEM((2, LANES, OWN), BF16),
        pltpu.VMEM((2, ALL, LANES), BF16),
        pltpu.VMEM((2, 2, C, OWN), BF16),
        pltpu.VMEM((4, 2, C, 128), BF16),
        pltpu.VMEM((ALL, 128), BF16),
    ]
    out_shape = (
        jax.ShapeDtypeStruct((LANES, OWN), BF16),
        jax.ShapeDtypeStruct((LANES, OWN), BF16),
        jax.ShapeDtypeStruct((27 * C, C), F32),
        jax.ShapeDtypeStruct((27 * C, C), F32),
    )
    arguments = (
        brick_list,
        features.reshape(LANES, OWN),
        cotangent.reshape(LANES, OWN),
        weight_one.reshape(27 * C, C),
        weight_two.reshape(27 * C, C),
    )
    results = pl.pallas_call(
        functools.partial(kernel, n_gx, n_gy, factor),
        out_shape=tuple(pltpu.VMEM(result.shape, result.dtype) for result in out_shape),
        in_specs=[pl.BlockSpec(memory_space=pltpu.HBM)] * 5,
        out_specs=[vmem] * 4,
        scratch_shapes=halo
        + halo
        + [
            pltpu.VMEM((2, 27, C, 128), BF16),
            pltpu.VMEM((2, 3, LANES, 3 * LANES), BF16),
            pltpu.VMEM((2, 3, 128, 3 * LANES), BF16),
            pltpu.VMEM((2, 3, LANES, 3 * 128), BF16),
            pltpu.VMEM((PACKED, 128), F32),
            pltpu.VMEM((n_plane, share, 128), F32),
            pltpu.VMEM((n_line, share, 128), BF16),
            pltpu.VMEM((PACKED, 128), F32),
        ]
        + [
            pltpu.SMEM((1, 1, BRICKS), jnp.int32),
            pltpu.VMEM((2, LANES, OWN), BF16),
            pltpu.VMEM((2, 27 * C, C), BF16),
        ]
        + [pltpu.SemaphoreType.DMA] * 15,
        compiler_params=pltpu.CompilerParams(
            collective_id=0, has_side_effects=True, vmem_limit_bytes=40 * 1024 * 1024
        ),
    )(*[pltpu.with_memory_space_constraint(value, pltpu.HBM) for value in arguments])
    block_out, grad_features, one, two = pl.pallas_call(
        deliver,
        out_shape=out_shape,
        in_specs=[vmem] * 4,
        out_specs=[pl.BlockSpec(memory_space=pl.ANY)] * 4,
        scratch_shapes=[pltpu.SemaphoreType.DMA] * 4,
    )(*results)
    flat = (C, SIDE, OWN)
    cube = (3, 3, 3, C, C)
    return block_out.reshape(flat), grad_features.reshape(flat), one.reshape(cube), two.reshape(cube)


def solution(mesh):
    return jax.shard_map(
        per_device,
        mesh=mesh,
        in_specs=(P(None, "gx", "gy"), P("gx", "gy", None), P(), P(), P(None, "gx", "gy")),
        out_specs=(P(None, "gx", "gy"), P(None, "gx", "gy"), P(), P()),
        check_vma=False,
    )
```

```python
import functools

import jax
import jax.numpy as jnp
from jax import lax
from jax.experimental import pallas as pl
from jax.experimental.pallas import tpu as pltpu
from jax.sharding import PartitionSpec as P

C = 32
SIDE = 8
NZ = 48
BRICKS = 6
LANES = SIDE * C
OWN = SIDE * NZ
ALL = OWN + 2 * NZ
PACKED = 512
X_HI = 2
MESH = pl.DeviceIdType.MESH
F32 = jnp.float32
BF16 = jnp.bfloat16


def dot(a, b, contract=((1,), (0,))):
    return lax.dot_general(a, b, (contract, ((), ())), preferred_element_type=F32)


def rows_mask(zero_at):
    z = lax.broadcasted_iota(jnp.int32, (NZ, LANES), 0)
    return jnp.concatenate([jnp.where(z == zero_at, 0.0, 1.0).astype(F32)] * SIDE, axis=0)


def from_below(value):
    return pltpu.roll(value, 1, 0) * rows_mask(0)


def from_above(value):
    return pltpu.roll(value, OWN - 1, 0) * rows_mask(NZ - 1)


def at(kx, ky, kz):
    return kx * 9 + ky * 3 + kz


def lane_block(shape=(C, 128)):
    return lax.broadcasted_iota(jnp.int32, shape, 1) // C


def widen_weights(w_ref, quad, which):
    lane = lax.broadcasted_iota(jnp.int32, (C, 128), 1)
    row = lax.broadcasted_iota(jnp.int32, (C, 128), 0)
    repeat = jnp.where(lane % C == row, 1.0, 0.0).astype(BF16)
    quad[which] = dot(w_ref[which], repeat).astype(BF16).reshape(27, C, 128)


def build_bands(quad, band, rim_in, rim_out):
    blocks = lane_block()
    masks = [jnp.where(blocks == b, 1.0, 0.0).astype(BF16) for b in range(4)]
    zero = jnp.zeros((C, 128), BF16)

    def step(i, carry):
        w, ky = i // 3, lax.rem(i, 3)
        rim_in[w, ky] = jnp.zeros((128, 3 * LANES), BF16)
        rim_out[w, ky] = jnp.zeros((LANES, 3 * 128), BF16)
        for kz in range(3):
            parts = [quad[w, at(kx, ky, kz)] for kx in range(3)]
            for xi in range(SIDE):
                for tile in range(2):
                    value = None
                    for kx in range(3):
                        xo = xi + 1 - kx - 4 * tile
                        if 0 <= xo < 4:
                            term = parts[kx] * masks[xo]
                            value = term if value is None else value + term
                    lanes = pl.ds(kz * LANES + tile * 128, 128)
                    band[w, ky, pl.ds(xi * C, C), lanes] = zero if value is None else value
            rim_in[w, ky, pl.ds(0, C), pl.ds(kz * LANES, 128)] = parts[0] * masks[0]
            rim_in[w, ky, pl.ds(C, C), pl.ds(kz * LANES + 128, 128)] = parts[2] * masks[3]
            rim_out[w, ky, pl.ds(0, C), pl.ds(kz * 128, 128)] = parts[2] * masks[2]
            rim_out[w, ky, pl.ds(LANES - C, C), pl.ds(kz * 128, 128)] = parts[0] * masks[3]
        return carry

    lax.fori_loop(0, 6, step, 0)


def shifted_rows(cells, rim, field):
    parts = [cells[field, pl.ds(ky * NZ, OWN), :] for ky in range(3)]
    return jnp.concatenate(parts + [rim[pl.ds(ky * NZ, OWN), :] for ky in range(3)], axis=1)


def conv_forward(cells, rim, band, rim_in, w):
    lhs = shifted_rows(cells, rim, 0)
    terms = []
    for kz in range(3):
        lanes = pl.ds(kz * LANES, LANES)
        rhs = jnp.concatenate(
            [band[w, ky, :, lanes] for ky in range(3)]
            + [rim_in[w, ky, :, lanes] for ky in range(3)],
            axis=0,
        )
        terms.append(dot(lhs, rhs))
    return terms[1] + from_below(terms[0]) + from_above(terms[2])


def conv_backward(cells, rim, band, rim_out, w):
    lhs = shifted_rows(cells, rim, 1)
    terms = []
    for kz in range(3):
        back = 2 - kz
        rhs = jnp.concatenate(
            [band[w, 2 - ky, :, pl.ds(back * LANES, LANES)] for ky in range(3)]
            + [rim_out[w, 2 - ky, :, pl.ds(back * 128, 128)] for ky in range(3)],
            axis=1,
        )
        terms.append(dot(lhs, rhs, ((1,), (1,))))
    return terms[1] + from_below(terms[0]) + from_above(terms[2])


def kernel_sums(own, cells, rim, field):
    wide = own.astype(F32)
    turned = {
        -1: from_above(wide).astype(BF16).T,
        0: own.T,
        1: from_below(wide).astype(BF16).T,
    }
    tall = jnp.concatenate([turned[sz] for sz in (-1, 0, 1)], axis=0)
    ends = jnp.concatenate(
        [turned[sz][part] for sz in (-1, 0, 1) for part in (slice(0, C), slice(LANES - C, LANES))],
        axis=0,
    )
    blocks = lane_block()
    sums = {}
    for sy in (-1, 0, 1):
        rows = pl.ds((1 + sy) * NZ, OWN)
        main = dot(tall, cells[field, rows, :])
        edge = dot(ends, rim[rows, :])
        for n, sz in enumerate((-1, 0, 1)):
            for sx in (-1, 0, 1):
                halves = []
                for tile in range(2):
                    value = None
                    for b in range(4):
                        a = 4 * tile + b - sx
                        if 0 <= a < SIDE:
                            top = n * LANES + a * C
                            term = main[top : top + C, tile * 128 : tile * 128 + 128]
                        else:
                            term = jnp.zeros((C, 128), F32)
                        value = term if value is None else jnp.where(blocks >= b, term, value)
                    halves.append(value)
                total = halves[0] + halves[1]
                if sx == -1:
                    total = total + jnp.where(blocks == 2 * field, edge[n * 64 : n * 64 + C], 0.0)
                if sx == 1:
                    total = total + jnp.where(
                        blocks == 2 * field + 1, edge[n * 64 + C : n * 64 + 64], 0.0
                    )
                sums[sx, sy, sz] = total
    return sums


def fold_four(a, b, c, d):
    blocks = lane_block()
    low = blocks < 2
    middle = (blocks == 1) | (blocks == 2)
    even = (blocks == 0) | (blocks == 2)
    ac = jnp.where(low, a, c) + pltpu.roll(jnp.where(low, c, a), 64, 1)
    bd = jnp.where(middle, b, d) + pltpu.roll(jnp.where(middle, d, b), 64, 1)
    return jnp.where(even, ac, bd) + pltpu.roll(jnp.where(even, bd, ac), 96, 1)


def kernel(
    n_gx, n_gy, factor,
    list_any, f_any, g_any, w1_any, w2_any,
    block_ref, back_ref, one_ref, two_ref,
    turned_a, cells_a, side_a, corner_a, rim_a,
    turned_b, cells_b, side_b, corner_b, rim_b,
    quad, band, rim_in, rim_out,
    packed, gathered, column, total,
    list_ref, fields_in, weights_in,
    list_sem, f_sem, g_sem, w1_sem, w2_sem,
    halo_send_a, halo_recv_a, halo_send_b, halo_recv_b,
    part_send, part_recv, line_send, line_recv, full_send, full_recv,
):
    gx, gy = lax.axis_index("gx"), lax.axis_index("gy")
    n_line = n_gx // X_HI
    n_plane = X_HI * n_gy
    x_hi = jnp.where(gx >= n_line, 1, 0)
    line = gx - x_hi * n_line
    rank = x_hi * n_gy + gy
    share = PACKED // n_plane
    n_seats = n_plane // 2
    n_busy = -(-7 * C // share)
    seat = rank // 2
    half = rank - 2 * seat
    busy = seat < n_busy

    def wrapped(value, count):
        value = jnp.where(value >= count, value - count, value)
        return jnp.where(value < 0, value + count, value)

    def beside(dx, dy):
        return (wrapped(gx + dx, n_gx), wrapped(gy + dy, n_gy))

    def in_plane(other):
        hi = jnp.where(other >= n_gy, 1, 0)
        return (hi * n_line + line, other - hi * n_gy)

    def in_line(other):
        return (x_hi * n_line + other, gy)

    barrier = pltpu.get_barrier_semaphore()
    around = [(dx, dy) for dx in (-1, 0, 1) for dy in (-1, 0, 1) if (dx, dy) != (0, 0)]
    def greet_plane(d, carry):
        target = in_plane(wrapped(rank + d, n_plane))
        pl.semaphore_signal(barrier, inc=1, device_id=target, device_id_type=MESH)
        return carry

    def greet_line(d, carry):
        target = in_line(wrapped(line + d, n_line))
        pl.semaphore_signal(barrier, inc=1, device_id=target, device_id_type=MESH)
        return carry

    lax.fori_loop(1, n_line, greet_line, 0)
    lax.fori_loop(1, n_plane, greet_plane, 0)
    for dx, dy in around:
        pl.semaphore_signal(barrier, inc=1, device_id=beside(dx, dy), device_id_type=MESH)
    loads = [
        pltpu.make_async_copy(src, dst, sem)
        for src, dst, sem in (
            (list_any, list_ref, list_sem),
            (f_any, fields_in.at[0], f_sem),
            (g_any, fields_in.at[1], g_sem),
            (w1_any, weights_in.at[0], w1_sem),
            (w2_any, weights_in.at[1], w2_sem),
        )
    ]
    for load in loads:
        load.start()

    loads[0].wait()
    hits = []
    for brick in range(BRICKS):
        count = jnp.int32(0)
        for slot in range(BRICKS):
            count = count + jnp.where(list_ref[0, 0, slot] == brick, 1, 0)
        hits.append(count.astype(F32))
    occupied = jnp.concatenate(
        [jnp.full((8, LANES), hit, F32) for hit in hits] * SIDE, axis=0
    )
    brick_of = lax.rem(lax.broadcasted_iota(jnp.int32, (8, OWN), 1), NZ) // 8
    across = jnp.zeros((8, OWN), F32)
    for brick in range(BRICKS):
        across = across + jnp.where(brick_of == brick, hits[brick], 0.0)
    across = jnp.concatenate([across] * (LANES // 8), axis=0)

    row = lax.broadcasted_iota(jnp.int32, (LANES, LANES), 0)
    col = lax.broadcasted_iota(jnp.int32, (LANES, LANES), 1)
    order = jnp.where(col == (row % C) * SIDE + row // C, 1.0, 0.0).astype(BF16)
    reorder = jnp.where(row == (col % C) * SIDE + col // C, 1.0, 0.0).astype(BF16)
    for field in range(2):
        loads[1 + field].wait()
        value = (dot(order, fields_in[field]) * across).astype(BF16)
        turned_a[field] = value
        cells_a[field, pl.ds(NZ, OWN), :] = value.T

    pl.semaphore_wait(barrier, len(around) + n_plane - 1 + n_line - 1)

    def exchange(turned, cells, side, corner, send, recv):
        low, high = pl.ds(0, C), pl.ds(LANES - C, C)
        every, head, tail = pl.ds(0, OWN), pl.ds(0, 128), pl.ds(OWN - 128, 128)

        def strip(rows, lanes):
            return turned.at[:, rows, lanes]

        def slab(y):
            return cells.at[:, pl.ds((y + 1) * NZ, NZ), :]

        def remote_copy(src, dst, group, dx, dy):
            return pltpu.make_async_remote_copy(
                src_ref=src,
                dst_ref=dst,
                send_sem=send.at[group],
                recv_sem=recv.at[group],
                device_id=beside(dx, dy),
                device_id_type=MESH,
            )

        @pl.when(gx < n_gx - 1)
        def _():
            remote_copy(strip(high, tail), corner.at[0], 1, 1, 1).start()
            remote_copy(strip(high, head), corner.at[2], 1, 1, -1).start()
            remote_copy(strip(high, every), side.at[0], 1, 1, 0).start()

        @pl.when(gx > 0)
        def _():
            remote_copy(strip(low, tail), corner.at[1], 2, -1, 1).start()
            remote_copy(strip(low, head), corner.at[3], 2, -1, -1).start()
            remote_copy(strip(low, every), side.at[1], 2, -1, 0).start()

        remote_copy(slab(SIDE - 1), slab(-1), 0, 0, 1).start()
        remote_copy(slab(0), slab(SIDE), 0, 0, -1).start()

        slabs = turned.at[0, pl.ds(0, 2 * NZ * 2), pl.ds(0, 256)]
        strips = turned.at[0, pl.ds(0, 160), pl.ds(0, 256)]

        def wait_recv():
            remote_copy(slabs, slabs, 0, 0, 1).wait_recv()

            @pl.when(gx > 0)
            def _():
                remote_copy(strips, strips, 1, 1, 0).wait_recv()

            @pl.when(gx < n_gx - 1)
            def _():
                remote_copy(strips, strips, 2, 1, 0).wait_recv()

        def wait_send():
            remote_copy(slabs, slabs, 0, 0, 1).wait_send()

            @pl.when(gx < n_gx - 1)
            def _():
                remote_copy(strips, strips, 1, 1, 0).wait_send()

            @pl.when(gx > 0)
            def _():
                remote_copy(strips, strips, 2, 1, 0).wait_send()

        return wait_recv, wait_send

    def place_rims(copies, cells, side, corner, rim):
        copies[0]()
        first_y, last_y = gy > 0, gy < n_gy - 1
        for rows, keep in ((pl.ds(0, NZ), first_y), (pl.ds(ALL - NZ, NZ), last_y)):
            for field in range(2):
                kept = jnp.where(keep, cells[field, rows, :].astype(F32), 0.0)
                cells[field, rows, :] = kept.astype(BF16)
        odd = lax.rem(lane_block((1, 128)), 2)
        inside = jnp.where(odd == 1, jnp.where(gx < n_gx - 1, 1, 0), jnp.where(gx > 0, 1, 0))

        def turn(left, right, keep):
            parts = [left[0], right[0], left[1], right[1]]
            value = jnp.concatenate(parts, axis=0).T.astype(F32)
            return jnp.where(inside * jnp.where(keep, 1, 0) > 0, value, 0.0).astype(BF16)

        rim[pl.ds(NZ, OWN), :] = turn(side[0], side[1], True)
        rim[pl.ds(0, NZ), :] = turn(corner[0], corner[1], first_y)[128 - NZ :]
        rim[pl.ds(ALL - NZ, NZ), :] = turn(corner[2], corner[3], last_y)[:NZ]

    copies_a = exchange(turned_a, cells_a, side_a, corner_a, halo_send_a, halo_recv_a)
    for w in range(2):
        loads[3 + w].wait()
        widen_weights(weights_in, quad, w)
    build_bands(quad, band, rim_in, rim_out)
    place_rims(copies_a, cells_a, side_a, corner_a, rim_a)

    pre_one = conv_forward(cells_a, rim_a, band, rim_in, 0) * occupied
    sigma = jax.nn.sigmoid(pre_one)
    hidden = (pre_one * sigma).astype(BF16)
    slope = occupied * sigma * (1.0 + pre_one * (1.0 - sigma))
    delta = (conv_backward(cells_a, rim_a, band, rim_out, 1) * slope).astype(BF16)
    for field, value in enumerate((hidden, delta)):
        cells_b[field, pl.ds(NZ, OWN), :] = value
        turned_b[field] = value.T

    def share_of(ref, other):
        other_seat = other // 2
        top = (other - 2 * other_seat) * (PACKED // 2) + other_seat * share
        return ref.at[pl.ds(pl.multiple_of(top, share), share), :]

    def remote(src, dst, send, recv, device):
        return pltpu.make_async_remote_copy(
            src_ref=src,
            dst_ref=dst,
            send_sem=send,
            recv_sem=recv,
            device_id=device,
            device_id_type=MESH,
        )

    def part_copy(target):
        src, dst = share_of(packed, target), gathered.at[rank]
        return remote(src, dst, part_send, part_recv, in_plane(target))

    def line_copy(target):
        src, dst = column.at[line], column.at[line]
        return remote(src, dst, line_send, line_recv, in_line(target))

    def full_copy(target):
        src, dst = share_of(total, rank), share_of(total, rank)
        return remote(src, dst, full_send, full_recv, in_plane(target))

    def start_parts(which):
        def step(d, carry):
            other = wrapped(seat + d, n_seats)

            @pl.when((other < n_busy) & (2 * other + which != rank))
            def _():
                part_copy(2 * other + which).start()

            return carry

        lax.fori_loop(0, n_seats, step, 0)

    def start_all(make, me, count):
        def step(d, carry):
            make(wrapped(me + d, count)).start()
            return carry

        lax.fori_loop(1, count, step, 0)

    def whole(ref, count, send, recv):
        part = ref.at[pl.ds(0, count)]
        return remote(part, part, send, recv, beside(1, 0))

    part_all = whole(gathered, n_plane - 1, part_send, part_recv)
    line_all = whole(column, n_line - 1, line_send, line_recv)

    def when_busy(busy_act, idle_act):
        pl.when(busy)(busy_act)
        if n_busy < n_seats:
            pl.when(jnp.logical_not(busy))(idle_act)

    def nothing():
        pass

    def wait_parts_sent():
        sent = 2 * n_busy
        when_busy(
            whole(gathered, sent - 1, part_send, part_recv).wait_send,
            whole(gathered, sent, part_send, part_recv).wait_send,
        )

    def wait_full():
        landed = 2 * n_busy * share
        when_busy(
            whole(total, landed - share, full_send, full_recv).wait_recv,
            whole(total, landed, full_send, full_recv).wait_recv,
        )

    def wait_full_sent():
        when_busy(
            whole(total, (n_plane - 1) * share, full_send, full_recv).wait_send, nothing
        )

    def summed(ref, count):
        value = ref[0].astype(F32)
        for n in range(1, count):
            value = value + ref[n].astype(F32)
        return value

    offsets = [(kx, ky, kz) for kx in (-1, 0, 1) for ky in (-1, 0, 1) for kz in (-1, 0, 1)]
    for which, own, field, sign in ((0, hidden, 1, -1), (1, delta, 0, 1)):
        sums = kernel_sums(own, cells_a, rim_a, field)
        parts = [sums[tuple(sign * o for o in offset)] for offset in offsets]
        parts.append(jnp.zeros((C, 128), F32))
        top = which * (PACKED // 2)
        for n, first in enumerate(range(0, 28, 4)):
            packed[pl.ds(top + n * C, C), :] = fold_four(*parts[first : first + 4])
        packed[pl.ds(top + 7 * C, C), :] = jnp.zeros((C, 128), F32)
        start_parts(which)

    copies_b = exchange(turned_b, cells_b, side_b, corner_b, halo_send_b, halo_recv_b)

    @pl.when(busy)
    def _():
        gathered[rank] = share_of(packed, rank)[...]
        part_all.wait_recv()
        column[line] = summed(gathered, n_plane).astype(BF16)
        start_all(line_copy, line, n_line)

    place_rims(copies_b, cells_b, side_b, corner_b, rim_b)
    pre_two = conv_forward(cells_b, rim_b, band, rim_in, 1) * occupied
    middle = pl.ds(NZ, OWN)
    block_out = (cells_a[0, middle, :].astype(F32) + pre_two).astype(BF16)
    block_ref[...] = dot(reorder, block_out, ((1,), (1,))).astype(BF16)
    back = conv_backward(cells_b, rim_b, band, rim_out, 0) * occupied
    grad_features = (cells_a[1, middle, :].astype(F32) + back).astype(BF16)
    back_ref[...] = dot(reorder, grad_features, ((1,), (1,))).astype(BF16)

    @pl.when(busy)
    def _():
        line_all.wait_recv()
        share_of(total, rank)[...] = summed(column, n_line).astype(BF16)
        start_all(full_copy, rank, n_plane)

    copies_a[1]()
    copies_b[1]()
    wait_parts_sent()
    pl.when(busy)(line_all.wait_send)
    wait_full()

    for n, first in enumerate(range(0, 27, 4)):
        count = min(4, 27 - first)
        one_ref[pl.ds(first * C, count * C), :] = (
            total[pl.ds(PACKED // 2 + n * C, C), :].astype(F32).T[: count * C] * factor
        )
        group = total[pl.ds(n * C, C), :].astype(F32) * factor
        for k in range(count):
            two_ref[pl.ds((first + k) * C, C), :] = group[:, k * C : (k + 1) * C]
    wait_full_sent()


def deliver(*refs):
    results, outs, sems = refs[:4], refs[4:8], refs[8:]
    copies = [pltpu.make_async_copy(*part) for part in zip(results, outs, sems)]
    for copy in copies:
        copy.start()
    for copy in copies:
        copy.wait()


def per_device(features, brick_list, weight_one, weight_two, cotangent):
    n_gx, n_gy = lax.axis_size("gx"), lax.axis_size("gy")
    n_line, n_plane = n_gx // X_HI, X_HI * n_gy
    share = PACKED // n_plane
    factor = float(n_gx * SIDE * n_gy * SIDE * NZ) ** (-0.5)
    vmem = pl.BlockSpec(memory_space=pltpu.VMEM)
    halo = [
        pltpu.VMEM((2, LANES, OWN), BF16),
        pltpu.VMEM((2, ALL, LANES), BF16),
        pltpu.VMEM((2, 2, C, OWN), BF16),
        pltpu.VMEM((4, 2, C, 128), BF16),
        pltpu.VMEM((ALL, 128), BF16),
    ]
    out_shape = (
        jax.ShapeDtypeStruct((LANES, OWN), BF16),
        jax.ShapeDtypeStruct((LANES, OWN), BF16),
        jax.ShapeDtypeStruct((27 * C, C), F32),
        jax.ShapeDtypeStruct((27 * C, C), F32),
    )
    arguments = (
        brick_list,
        features.reshape(LANES, OWN),
        cotangent.reshape(LANES, OWN),
        weight_one.reshape(27 * C, C),
        weight_two.reshape(27 * C, C),
    )
    results = pl.pallas_call(
        functools.partial(kernel, n_gx, n_gy, factor),
        out_shape=tuple(pltpu.VMEM(result.shape, result.dtype) for result in out_shape),
        in_specs=[pl.BlockSpec(memory_space=pltpu.HBM)] * 5,
        out_specs=[vmem] * 4,
        scratch_shapes=halo
        + halo
        + [
            pltpu.VMEM((2, 27, C, 128), BF16),
            pltpu.VMEM((2, 3, LANES, 3 * LANES), BF16),
            pltpu.VMEM((2, 3, 128, 3 * LANES), BF16),
            pltpu.VMEM((2, 3, LANES, 3 * 128), BF16),
            pltpu.VMEM((PACKED, 128), F32),
            pltpu.VMEM((n_plane, share, 128), F32),
            pltpu.VMEM((n_line, share, 128), BF16),
            pltpu.VMEM((PACKED, 128), BF16),
        ]
        + [
            pltpu.SMEM((1, 1, BRICKS), jnp.int32),
            pltpu.VMEM((2, LANES, OWN), BF16),
            pltpu.VMEM((2, 27 * C, C), BF16),
        ]
        + [pltpu.SemaphoreType.DMA] * 5
        + [pltpu.SemaphoreType.DMA((3,))] * 4
        + [pltpu.SemaphoreType.DMA] * 6,
        compiler_params=pltpu.CompilerParams(
            collective_id=0, has_side_effects=True, vmem_limit_bytes=40 * 1024 * 1024
        ),
    )(*[pltpu.with_memory_space_constraint(value, pltpu.HBM) for value in arguments])
    block_out, grad_features, one, two = pl.pallas_call(
        deliver,
        out_shape=out_shape,
        in_specs=[vmem] * 4,
        out_specs=[pl.BlockSpec(memory_space=pl.ANY)] * 4,
        scratch_shapes=[pltpu.SemaphoreType.DMA] * 4,
        compiler_params=pltpu.CompilerParams(vmem_limit_bytes=4 * 1024 * 1024),
    )(*[pltpu.with_memory_space_constraint(value, pltpu.VMEM) for value in results])
    flat = (C, SIDE, OWN)
    cube = (3, 3, 3, C, C)
    return block_out.reshape(flat), grad_features.reshape(flat), one.reshape(cube), two.reshape(cube)


def solution(mesh):
    return jax.shard_map(
        per_device,
        mesh=mesh,
        in_specs=(P(None, "gx", "gy"), P("gx", "gy", None), P(), P(), P(None, "gx", "gy")),
        out_specs=(P(None, "gx", "gy"), P(None, "gx", "gy"), P(), P()),
        check_vma=False,
    )
```

```python
import functools

import jax
import jax.numpy as jnp
from jax import lax
from jax.experimental import pallas as pl
from jax.experimental.pallas import tpu as pltpu
from jax.sharding import PartitionSpec as P

C = 32
SIDE = 8
NZ = 48
BRICKS = 6
LANES = SIDE * C
OWN = SIDE * NZ
ALL = OWN + 2 * NZ
PACKED = 512
PIECES = 4
X_HI = 2
X_LO = 2
CORES = 2
MESH = pl.DeviceIdType.MESH
F32 = jnp.float32
BF16 = jnp.bfloat16


def dot(a, b, contract=((1,), (0,))):
    return lax.dot_general(a, b, (contract, ((), ())), preferred_element_type=F32)


def rows_mask(zero_at):
    z = lax.broadcasted_iota(jnp.int32, (NZ, LANES), 0)
    return jnp.concatenate([jnp.where(z == zero_at, 0.0, 1.0).astype(F32)] * SIDE, axis=0)


def from_below(value):
    return pltpu.roll(value, 1, 0) * rows_mask(0)


def from_above(value):
    return pltpu.roll(value, OWN - 1, 0) * rows_mask(NZ - 1)


def at(kx, ky, kz):
    return kx * 9 + ky * 3 + kz


def lane_block(shape=(C, 128)):
    return lax.broadcasted_iota(jnp.int32, shape, 1) // C


def widen_weights(w_ref, quad, which):
    lane = lax.broadcasted_iota(jnp.int32, (C, 128), 1)
    row = lax.broadcasted_iota(jnp.int32, (C, 128), 0)
    repeat = jnp.where(lane % C == row, 1.0, 0.0).astype(BF16)
    quad[which] = dot(w_ref[which], repeat).astype(BF16).reshape(27, C, 128)


def build_bands(quad, band, rim_in, rim_out):
    blocks = lane_block()
    masks = [jnp.where(blocks == b, 1.0, 0.0).astype(BF16) for b in range(4)]
    zero = jnp.zeros((C, 128), BF16)

    def step(i, carry):
        w, ky = i // 3, lax.rem(i, 3)
        rim_in[w, ky] = jnp.zeros((128, 3 * LANES), BF16)
        rim_out[w, ky] = jnp.zeros((LANES, 3 * 128), BF16)
        for kz in range(3):
            parts = [quad[w, at(kx, ky, kz)] for kx in range(3)]
            for xi in range(SIDE):
                for tile in range(2):
                    value = None
                    for kx in range(3):
                        xo = xi + 1 - kx - 4 * tile
                        if 0 <= xo < 4:
                            term = parts[kx] * masks[xo]
                            value = term if value is None else value + term
                    lanes = pl.ds(kz * LANES + tile * 128, 128)
                    band[w, ky, pl.ds(xi * C, C), lanes] = zero if value is None else value
            rim_in[w, ky, pl.ds(0, C), pl.ds(kz * LANES, 128)] = parts[0] * masks[0]
            rim_in[w, ky, pl.ds(C, C), pl.ds(kz * LANES + 128, 128)] = parts[2] * masks[3]
            rim_out[w, ky, pl.ds(0, C), pl.ds(kz * 128, 128)] = parts[2] * masks[2]
            rim_out[w, ky, pl.ds(LANES - C, C), pl.ds(kz * 128, 128)] = parts[0] * masks[3]
        return carry

    lax.fori_loop(0, 6, step, 0)


def shifted_rows(cells, rim, field):
    parts = [cells[field, pl.ds(ky * NZ, OWN), :] for ky in range(3)]
    return jnp.concatenate(parts + [rim[pl.ds(ky * NZ, OWN), :] for ky in range(3)], axis=1)


def conv_forward(cells, rim, band, rim_in, w):
    lhs = shifted_rows(cells, rim, 0)
    terms = []
    for kz in range(3):
        lanes = pl.ds(kz * LANES, LANES)
        rhs = jnp.concatenate(
            [band[w, ky, :, lanes] for ky in range(3)]
            + [rim_in[w, ky, :, lanes] for ky in range(3)],
            axis=0,
        )
        terms.append(dot(lhs, rhs))
    return terms[1] + from_below(terms[0]) + from_above(terms[2])


def conv_backward(cells, rim, band, rim_out, w):
    lhs = shifted_rows(cells, rim, 1)
    terms = []
    for kz in range(3):
        back = 2 - kz
        rhs = jnp.concatenate(
            [band[w, 2 - ky, :, pl.ds(back * LANES, LANES)] for ky in range(3)]
            + [rim_out[w, 2 - ky, :, pl.ds(back * 128, 128)] for ky in range(3)],
            axis=1,
        )
        terms.append(dot(lhs, rhs, ((1,), (1,))))
    return terms[1] + from_below(terms[0]) + from_above(terms[2])


def kernel_sums(own, cells, rim, field):
    wide = own.astype(F32)
    turned = {
        -1: from_above(wide).astype(BF16).T,
        0: own.T,
        1: from_below(wide).astype(BF16).T,
    }
    tall = jnp.concatenate([turned[sz] for sz in (-1, 0, 1)], axis=0)
    ends = jnp.concatenate(
        [turned[sz][part] for sz in (-1, 0, 1) for part in (slice(0, C), slice(LANES - C, LANES))],
        axis=0,
    )
    blocks = lane_block()
    sums = {}
    for sy in (-1, 0, 1):
        rows = pl.ds((1 + sy) * NZ, OWN)
        main = dot(tall, cells[field, rows, :])
        edge = dot(ends, rim[rows, :])
        for n, sz in enumerate((-1, 0, 1)):
            for sx in (-1, 0, 1):
                halves = []
                for tile in range(2):
                    value = None
                    for b in range(4):
                        a = 4 * tile + b - sx
                        if 0 <= a < SIDE:
                            top = n * LANES + a * C
                            term = main[top : top + C, tile * 128 : tile * 128 + 128]
                        else:
                            term = jnp.zeros((C, 128), F32)
                        value = term if value is None else jnp.where(blocks >= b, term, value)
                    halves.append(value)
                total = halves[0] + halves[1]
                if sx == -1:
                    total = total + jnp.where(blocks == 2 * field, edge[n * 64 : n * 64 + C], 0.0)
                if sx == 1:
                    total = total + jnp.where(
                        blocks == 2 * field + 1, edge[n * 64 + C : n * 64 + 64], 0.0
                    )
                sums[sx, sy, sz] = total
    return sums


def fold_four(a, b, c, d):
    blocks = lane_block()
    low = blocks < 2
    middle = (blocks == 1) | (blocks == 2)
    even = (blocks == 0) | (blocks == 2)
    ac = jnp.where(low, a, c) + pltpu.roll(jnp.where(low, c, a), 64, 1)
    bd = jnp.where(middle, b, d) + pltpu.roll(jnp.where(middle, d, b), 64, 1)
    return jnp.where(even, ac, bd) + pltpu.roll(jnp.where(even, bd, ac), 96, 1)


def kernel(
    n_gx, n_gy, factor,
    list_any, f_any, g_any, w1_any, w2_any,
    block_ref, back_ref, one_ref, two_ref,
    turned_a, cells_a, side_a, corner_a, rim_a,
    turned_b, cells_b, side_b, corner_b, rim_b,
    quad, band, rim_in, rim_out,
    packed, gathered, column, total,
    list_ref, fields_in, weights_in,
    list_sem, f_sem, g_sem, w1_sem, w2_sem,
    halo_send_a, halo_recv_a, halo_send_b, halo_recv_b,
    part_send, part_recv, line_send, line_recv, full_send, full_recv,
):
    gx, gy = lax.axis_index("gx"), lax.axis_index("gy")
    n_line = n_gx // X_HI
    n_plane = X_HI * n_gy
    x_hi = jnp.where(gx >= n_line, 1, 0)
    line = gx - x_hi * n_line
    rank = x_hi * n_gy + gy
    share = PACKED // n_plane
    n_seats = n_plane // 2
    n_busy = -(-7 * C // share)
    seat = rank // 2
    half = rank - 2 * seat
    busy = seat < n_busy

    def wrapped(value, count):
        value = jnp.where(value >= count, value - count, value)
        return jnp.where(value < 0, value + count, value)

    def beside(dx, dy):
        return (wrapped(gx + dx, n_gx), wrapped(gy + dy, n_gy))

    def in_plane(other):
        hi = jnp.where(other >= n_gy, 1, 0)
        return (hi * n_line + line, other - hi * n_gy)

    def in_line(other):
        return (x_hi * n_line + other, gy)

    n_x, n_y = X_HI * X_LO, n_gy // (X_LO * CORES)
    y = gy // (X_LO * CORES)
    x = x_hi * X_LO + gy // CORES - y * X_LO

    def hops(offset, count):
        return min(offset, count - offset)

    chips = [(dy, dx) for dy in range(n_y) for dx in range(n_x)]
    chips.sort(key=lambda chip: -hops(chip[0], n_y) - hops(chip[1], n_x))
    steps = sorted(range(1, n_line), key=lambda d: -hops(d, n_line))

    def seat_at(dy, dx):
        other_y, other_x = wrapped(y + dy, n_y), wrapped(x + dx, n_x)
        hi = jnp.where(other_x >= X_LO, 1, 0)
        return hi * (n_seats - n_seats // X_HI) + other_y * X_LO + other_x - hi * X_LO

    barrier = pltpu.get_barrier_semaphore()
    around = [(dx, dy) for dx in (-1, 0, 1) for dy in (-1, 0, 1) if (dx, dy) != (0, 0)]
    for d in steps:
        target = in_line(wrapped(line + d, n_line))
        pl.semaphore_signal(barrier, inc=1, device_id=target, device_id_type=MESH)
    for chip in chips:
        for core in range(CORES):
            if chip != (0, 0):
                target = in_plane(2 * seat_at(*chip) + core)
                pl.semaphore_signal(barrier, inc=1, device_id=target, device_id_type=MESH)
    target = in_plane(2 * seat + 1 - half)
    pl.semaphore_signal(barrier, inc=1, device_id=target, device_id_type=MESH)
    for dx, dy in around:
        pl.semaphore_signal(barrier, inc=1, device_id=beside(dx, dy), device_id_type=MESH)
    loads = [
        pltpu.make_async_copy(src, dst, sem)
        for src, dst, sem in (
            (list_any, list_ref, list_sem),
            (f_any, fields_in.at[0], f_sem),
            (g_any, fields_in.at[1], g_sem),
            (w1_any, weights_in.at[0], w1_sem),
            (w2_any, weights_in.at[1], w2_sem),
        )
    ]
    for load in loads:
        load.start()

    loads[0].wait()
    hits = []
    for brick in range(BRICKS):
        count = jnp.int32(0)
        for slot in range(BRICKS):
            count = count + jnp.where(list_ref[0, 0, slot] == brick, 1, 0)
        hits.append(count.astype(F32))
    occupied = jnp.concatenate(
        [jnp.full((8, LANES), hit, F32) for hit in hits] * SIDE, axis=0
    )
    brick_of = lax.rem(lax.broadcasted_iota(jnp.int32, (8, OWN), 1), NZ) // 8
    across = jnp.zeros((8, OWN), F32)
    for brick in range(BRICKS):
        across = across + jnp.where(brick_of == brick, hits[brick], 0.0)
    across = jnp.concatenate([across] * (LANES // 8), axis=0)

    row = lax.broadcasted_iota(jnp.int32, (LANES, LANES), 0)
    col = lax.broadcasted_iota(jnp.int32, (LANES, LANES), 1)
    order = jnp.where(col == (row % C) * SIDE + row // C, 1.0, 0.0).astype(BF16)
    reorder = jnp.where(row == (col % C) * SIDE + col // C, 1.0, 0.0).astype(BF16)
    for field in range(2):
        loads[1 + field].wait()
        value = (dot(order, fields_in[field]) * across).astype(BF16)
        turned_a[field] = value
        cells_a[field, pl.ds(NZ, OWN), :] = value.T

    pl.semaphore_wait(barrier, len(around) + n_plane - 1 + n_line - 1)

    def exchange(turned, cells, side, corner, send, recv):
        low, high = pl.ds(0, C), pl.ds(LANES - C, C)
        every, head, tail = pl.ds(0, OWN), pl.ds(0, 128), pl.ds(OWN - 128, 128)

        def strip(rows, lanes):
            return turned.at[:, rows, lanes]

        def slab(y):
            return cells.at[:, pl.ds((y + 1) * NZ, NZ), :]

        def remote_copy(src, dst, group, dx, dy):
            return pltpu.make_async_remote_copy(
                src_ref=src,
                dst_ref=dst,
                send_sem=send.at[group],
                recv_sem=recv.at[group],
                device_id=beside(dx, dy),
                device_id_type=MESH,
            )

        @pl.when(gx < n_gx - 1)
        def _():
            remote_copy(strip(high, tail), corner.at[0], 1, 1, 1).start()
            remote_copy(strip(high, head), corner.at[2], 1, 1, -1).start()
            remote_copy(strip(high, every), side.at[0], 1, 1, 0).start()

        @pl.when(gx > 0)
        def _():
            remote_copy(strip(low, tail), corner.at[1], 2, -1, 1).start()
            remote_copy(strip(low, head), corner.at[3], 2, -1, -1).start()
            remote_copy(strip(low, every), side.at[1], 2, -1, 0).start()

        remote_copy(slab(SIDE - 1), slab(-1), 0, 0, 1).start()
        remote_copy(slab(0), slab(SIDE), 0, 0, -1).start()

        slabs = turned.at[0, pl.ds(0, 2 * NZ * 2), pl.ds(0, 256)]
        strips = turned.at[0, pl.ds(0, 160), pl.ds(0, 256)]

        def wait_recv():
            remote_copy(slabs, slabs, 0, 0, 1).wait_recv()

            @pl.when(gx > 0)
            def _():
                remote_copy(strips, strips, 1, 1, 0).wait_recv()

            @pl.when(gx < n_gx - 1)
            def _():
                remote_copy(strips, strips, 2, 1, 0).wait_recv()

        def wait_send():
            remote_copy(slabs, slabs, 0, 0, 1).wait_send()

            @pl.when(gx < n_gx - 1)
            def _():
                remote_copy(strips, strips, 1, 1, 0).wait_send()

            @pl.when(gx > 0)
            def _():
                remote_copy(strips, strips, 2, 1, 0).wait_send()

        return wait_recv, wait_send

    def place_rims(copies, cells, side, corner, rim):
        copies[0]()
        first_y, last_y = gy > 0, gy < n_gy - 1
        for rows, keep in ((pl.ds(0, NZ), first_y), (pl.ds(ALL - NZ, NZ), last_y)):
            for field in range(2):
                kept = jnp.where(keep, cells[field, rows, :].astype(F32), 0.0)
                cells[field, rows, :] = kept.astype(BF16)
        odd = lax.rem(lane_block((1, 128)), 2)
        inside = jnp.where(odd == 1, jnp.where(gx < n_gx - 1, 1, 0), jnp.where(gx > 0, 1, 0))

        def turn(left, right, keep):
            parts = [left[0], right[0], left[1], right[1]]
            value = jnp.concatenate(parts, axis=0).T.astype(F32)
            return jnp.where(inside * jnp.where(keep, 1, 0) > 0, value, 0.0).astype(BF16)

        rim[pl.ds(NZ, OWN), :] = turn(side[0], side[1], True)
        rim[pl.ds(0, NZ), :] = turn(corner[0], corner[1], first_y)[128 - NZ :]
        rim[pl.ds(ALL - NZ, NZ), :] = turn(corner[2], corner[3], last_y)[:NZ]

    copies_a = exchange(turned_a, cells_a, side_a, corner_a, halo_send_a, halo_recv_a)
    for w in range(2):
        loads[3 + w].wait()
        widen_weights(weights_in, quad, w)
    build_bands(quad, band, rim_in, rim_out)
    place_rims(copies_a, cells_a, side_a, corner_a, rim_a)

    pre_one = conv_forward(cells_a, rim_a, band, rim_in, 0) * occupied
    sigma = jax.nn.sigmoid(pre_one)
    hidden = (pre_one * sigma).astype(BF16)
    slope = occupied * sigma * (1.0 + pre_one * (1.0 - sigma))
    delta = (conv_backward(cells_a, rim_a, band, rim_out, 1) * slope).astype(BF16)
    for field, value in enumerate((hidden, delta)):
        cells_b[field, pl.ds(NZ, OWN), :] = value
        turned_b[field] = value.T

    def share_of(ref, other):
        other_seat = other // 2
        top = (other - 2 * other_seat) * (PACKED // 2) + other_seat * share
        return ref.at[pl.ds(pl.multiple_of(top, share), share), :]

    def remote(src, dst, send, recv, device):
        return pltpu.make_async_remote_copy(
            src_ref=src,
            dst_ref=dst,
            send_sem=send,
            recv_sem=recv,
            device_id=device,
            device_id_type=MESH,
        )

    def part_copy(target):
        src, dst = share_of(packed, target), gathered.at[rank]
        return remote(src, dst, part_send, part_recv, in_plane(target))

    def line_copy(target):
        src, dst = column.at[line], column.at[line]
        return remote(src, dst, line_send, line_recv, in_line(target))

    def full_copy(target):
        src, dst = share_of(total, rank), share_of(total, rank)
        return remote(src, dst, full_send, full_recv, in_plane(target))

    def start_parts(which):
        for chip in chips:
            other = seat_at(*chip)

            @pl.when((other < n_busy) & (2 * other + which != rank))
            def _():
                part_copy(2 * other + which).start()

    def start_line():
        for d in steps:
            line_copy(wrapped(line + d, n_line)).start()

    def start_full():
        for chip in chips:
            other = 2 * seat_at(*chip)
            for core in range(CORES):
                if chip == (0, 0):
                    continue
                full_copy(other + core).start()
        full_copy(2 * seat + 1 - half).start()

    def whole(ref, count, send, recv):
        part = ref.at[pl.ds(0, count)]
        return remote(part, part, send, recv, beside(1, 0))

    part_all = whole(gathered, n_plane - 1, part_send, part_recv)
    line_all = whole(column, n_line - 1, line_send, line_recv)

    def when_busy(busy_act, idle_act):
        pl.when(busy)(busy_act)
        if n_busy < n_seats:
            pl.when(jnp.logical_not(busy))(idle_act)

    def nothing():
        pass

    def wait_parts_sent():
        sent = 2 * n_busy
        when_busy(
            whole(gathered, sent - 1, part_send, part_recv).wait_send,
            whole(gathered, sent, part_send, part_recv).wait_send,
        )

    def wait_full():
        landed = 2 * n_busy * share
        when_busy(
            whole(total, landed - share, full_send, full_recv).wait_recv,
            whole(total, landed, full_send, full_recv).wait_recv,
        )

    def wait_full_sent():
        when_busy(
            whole(total, (n_plane - 1) * share, full_send, full_recv).wait_send, nothing
        )

    def summed(ref, count):
        value = ref[0].astype(F32)
        for n in range(1, count):
            value = value + ref[n].astype(F32)
        return value

    copies_b = exchange(turned_b, cells_b, side_b, corner_b, halo_send_b, halo_recv_b)
    offsets = [(kx, ky, kz) for kx in (-1, 0, 1) for ky in (-1, 0, 1) for kz in (-1, 0, 1)]
    for which, own, field, sign in ((0, hidden, 1, -1), (1, delta, 0, 1)):
        sums = kernel_sums(own, cells_a, rim_a, field)
        parts = [sums[tuple(sign * o for o in offset)] for offset in offsets]
        parts.append(jnp.zeros((C, 128), F32))
        top = which * (PACKED // 2)
        for n, first in enumerate(range(0, 28, 4)):
            packed[pl.ds(top + n * C, C), :] = fold_four(*parts[first : first + 4])
        packed[pl.ds(top + 7 * C, C), :] = jnp.zeros((C, 128), F32)
        start_parts(which)


    @pl.when(busy)
    def _():
        gathered[rank] = share_of(packed, rank)[...]
        part_all.wait_recv()
        column[line] = summed(gathered, n_plane).astype(BF16)
        start_line()

    place_rims(copies_b, cells_b, side_b, corner_b, rim_b)
    pre_two = conv_forward(cells_b, rim_b, band, rim_in, 1) * occupied
    middle = pl.ds(NZ, OWN)
    block_out = (cells_a[0, middle, :].astype(F32) + pre_two).astype(BF16)
    block_ref[...] = dot(reorder, block_out, ((1,), (1,))).astype(BF16)
    back = conv_backward(cells_b, rim_b, band, rim_out, 0) * occupied
    grad_features = (cells_a[1, middle, :].astype(F32) + back).astype(BF16)
    back_ref[...] = dot(reorder, grad_features, ((1,), (1,))).astype(BF16)

    @pl.when(busy)
    def _():
        line_all.wait_recv()
        share_of(total, rank)[...] = summed(column, n_line).astype(BF16)
        start_full()

    copies_a[1]()
    copies_b[1]()
    wait_parts_sent()
    pl.when(busy)(line_all.wait_send)
    wait_full()

    for n, first in enumerate(range(0, 27, 4)):
        count = min(4, 27 - first)
        one_ref[pl.ds(first * C, count * C), :] = (
            total[pl.ds(PACKED // 2 + n * C, C), :].astype(F32).T[: count * C] * factor
        )
        group = total[pl.ds(n * C, C), :].astype(F32) * factor
        for k in range(count):
            two_ref[pl.ds((first + k) * C, C), :] = group[:, k * C : (k + 1) * C]
    wait_full_sent()


def deliver(*refs):
    results, outs, sems = refs[:4], refs[4:8], refs[8]
    copies = []
    for n, (result, out) in enumerate(zip(results, outs)):
        rows = result.shape[0] // PIECES
        for piece in range(PIECES):
            part = pl.ds(piece * rows, rows)
            sem = sems.at[n, piece]
            copies.append(pltpu.make_async_copy(result.at[part], out.at[part], sem))
    for copy in copies:
        copy.start()
    for copy in copies:
        copy.wait()


def per_device(features, brick_list, weight_one, weight_two, cotangent):
    n_gx, n_gy = lax.axis_size("gx"), lax.axis_size("gy")
    n_line, n_plane = n_gx // X_HI, X_HI * n_gy
    share = PACKED // n_plane
    factor = float(n_gx * SIDE * n_gy * SIDE * NZ) ** (-0.5)
    vmem = pl.BlockSpec(memory_space=pltpu.VMEM)
    halo = [
        pltpu.VMEM((2, LANES, OWN), BF16),
        pltpu.VMEM((2, ALL, LANES), BF16),
        pltpu.VMEM((2, 2, C, OWN), BF16),
        pltpu.VMEM((4, 2, C, 128), BF16),
        pltpu.VMEM((ALL, 128), BF16),
    ]
    out_shape = (
        jax.ShapeDtypeStruct((LANES, OWN), BF16),
        jax.ShapeDtypeStruct((LANES, OWN), BF16),
        jax.ShapeDtypeStruct((27 * C, C), F32),
        jax.ShapeDtypeStruct((27 * C, C), F32),
    )
    arguments = (
        brick_list,
        features.reshape(LANES, OWN),
        cotangent.reshape(LANES, OWN),
        weight_one.reshape(27 * C, C),
        weight_two.reshape(27 * C, C),
    )
    results = pl.pallas_call(
        functools.partial(kernel, n_gx, n_gy, factor),
        out_shape=tuple(pltpu.VMEM(result.shape, result.dtype) for result in out_shape),
        in_specs=[pl.BlockSpec(memory_space=pltpu.HBM)] * 5,
        out_specs=[vmem] * 4,
        scratch_shapes=halo
        + halo
        + [
            pltpu.VMEM((2, 27, C, 128), BF16),
            pltpu.VMEM((2, 3, LANES, 3 * LANES), BF16),
            pltpu.VMEM((2, 3, 128, 3 * LANES), BF16),
            pltpu.VMEM((2, 3, LANES, 3 * 128), BF16),
            pltpu.VMEM((PACKED, 128), F32),
            pltpu.VMEM((n_plane, share, 128), F32),
            pltpu.VMEM((n_line, share, 128), BF16),
            pltpu.VMEM((PACKED, 128), BF16),
        ]
        + [
            pltpu.SMEM((1, 1, BRICKS), jnp.int32),
            pltpu.VMEM((2, LANES, OWN), BF16),
            pltpu.VMEM((2, 27 * C, C), BF16),
        ]
        + [pltpu.SemaphoreType.DMA] * 5
        + [pltpu.SemaphoreType.DMA((3,))] * 4
        + [pltpu.SemaphoreType.DMA] * 6,
        compiler_params=pltpu.CompilerParams(
            collective_id=0, has_side_effects=True, vmem_limit_bytes=40 * 1024 * 1024
        ),
    )(*[pltpu.with_memory_space_constraint(value, pltpu.HBM) for value in arguments])
    block_out, grad_features, one, two = pl.pallas_call(
        deliver,
        out_shape=out_shape,
        in_specs=[vmem] * 4,
        out_specs=[pl.BlockSpec(memory_space=pl.ANY)] * 4,
        scratch_shapes=[pltpu.SemaphoreType.DMA((4, PIECES))],
        compiler_params=pltpu.CompilerParams(vmem_limit_bytes=4 * 1024 * 1024),
    )(*[pltpu.with_memory_space_constraint(value, pltpu.VMEM) for value in results])
    flat = (C, SIDE, OWN)
    cube = (3, 3, 3, C, C)
    return block_out.reshape(flat), grad_features.reshape(flat), one.reshape(cube), two.reshape(cube)


def solution(mesh):
    return jax.shard_map(
        per_device,
        mesh=mesh,
        in_specs=(P(None, "gx", "gy"), P("gx", "gy", None), P(), P(), P(None, "gx", "gy")),
        out_specs=(P(None, "gx", "gy"), P(None, "gx", "gy"), P(), P()),
        check_vma=False,
    )
```

```python
import functools

import jax
import jax.numpy as jnp
from jax import lax
from jax.experimental import pallas as pl
from jax.experimental.pallas import tpu as pltpu
from jax.sharding import PartitionSpec as P

C = 32
SIDE = 8
NZ = 48
BRICKS = 6
LANES = SIDE * C
OWN = SIDE * NZ
ALL = OWN + 2 * NZ
PACKED = 512
PIECES = 4
X_HI = 2
REACH = 3
X_LO = 2
CORES = 2
MESH = pl.DeviceIdType.MESH
F32 = jnp.float32
BF16 = jnp.bfloat16


def dot(a, b, contract=((1,), (0,))):
    return lax.dot_general(a, b, (contract, ((), ())), preferred_element_type=F32)


def rows_mask(zero_at):
    z = lax.broadcasted_iota(jnp.int32, (NZ, LANES), 0)
    return jnp.concatenate([jnp.where(z == zero_at, 0.0, 1.0).astype(F32)] * SIDE, axis=0)


def from_below(value):
    return pltpu.roll(value, 1, 0) * rows_mask(0)


def from_above(value):
    return pltpu.roll(value, OWN - 1, 0) * rows_mask(NZ - 1)


def at(kx, ky, kz):
    return kx * 9 + ky * 3 + kz


def lane_block(shape=(C, 128)):
    return lax.broadcasted_iota(jnp.int32, shape, 1) // C


def widen_weights(w_ref, quad, which):
    lane = lax.broadcasted_iota(jnp.int32, (C, 128), 1)
    row = lax.broadcasted_iota(jnp.int32, (C, 128), 0)
    repeat = jnp.where(lane % C == row, 1.0, 0.0).astype(BF16)
    quad[which] = dot(w_ref[which], repeat).astype(BF16).reshape(27, C, 128)


def build_bands(quad, band, rim_in, rim_out):
    blocks = lane_block()
    masks = [jnp.where(blocks == b, 1.0, 0.0).astype(BF16) for b in range(4)]
    zero = jnp.zeros((C, 128), BF16)

    def step(i, carry):
        w, ky = i // 3, lax.rem(i, 3)
        rim_in[w, ky] = jnp.zeros((128, 3 * LANES), BF16)
        rim_out[w, ky] = jnp.zeros((LANES, 3 * 128), BF16)
        for kz in range(3):
            parts = [quad[w, at(kx, ky, kz)] for kx in range(3)]
            for xi in range(SIDE):
                for tile in range(2):
                    value = None
                    for kx in range(3):
                        xo = xi + 1 - kx - 4 * tile
                        if 0 <= xo < 4:
                            term = parts[kx] * masks[xo]
                            value = term if value is None else value + term
                    lanes = pl.ds(kz * LANES + tile * 128, 128)
                    band[w, ky, pl.ds(xi * C, C), lanes] = zero if value is None else value
            rim_in[w, ky, pl.ds(0, C), pl.ds(kz * LANES, 128)] = parts[0] * masks[0]
            rim_in[w, ky, pl.ds(C, C), pl.ds(kz * LANES + 128, 128)] = parts[2] * masks[3]
            rim_out[w, ky, pl.ds(0, C), pl.ds(kz * 128, 128)] = parts[2] * masks[2]
            rim_out[w, ky, pl.ds(LANES - C, C), pl.ds(kz * 128, 128)] = parts[0] * masks[3]
        return carry

    lax.fori_loop(0, 6, step, 0)


def shifted_rows(cells, rim, field):
    parts = [cells[field, pl.ds(ky * NZ, OWN), :] for ky in range(3)]
    return jnp.concatenate(parts + [rim[pl.ds(ky * NZ, OWN), :] for ky in range(3)], axis=1)


def conv_forward(cells, rim, band, rim_in, w):
    lhs = shifted_rows(cells, rim, 0)
    terms = []
    for kz in range(3):
        lanes = pl.ds(kz * LANES, LANES)
        rhs = jnp.concatenate(
            [band[w, ky, :, lanes] for ky in range(3)]
            + [rim_in[w, ky, :, lanes] for ky in range(3)],
            axis=0,
        )
        terms.append(dot(lhs, rhs))
    return terms[1] + from_below(terms[0]) + from_above(terms[2])


def conv_backward(cells, rim, band, rim_out, w):
    lhs = shifted_rows(cells, rim, 1)
    terms = []
    for kz in range(3):
        back = 2 - kz
        rhs = jnp.concatenate(
            [band[w, 2 - ky, :, pl.ds(back * LANES, LANES)] for ky in range(3)]
            + [rim_out[w, 2 - ky, :, pl.ds(back * 128, 128)] for ky in range(3)],
            axis=1,
        )
        terms.append(dot(lhs, rhs, ((1,), (1,))))
    return terms[1] + from_below(terms[0]) + from_above(terms[2])


def kernel_sums(own, cells, rim, field):
    wide = own.astype(F32)
    turned = {
        -1: from_above(wide).astype(BF16).T,
        0: own.T,
        1: from_below(wide).astype(BF16).T,
    }
    tall = jnp.concatenate([turned[sz] for sz in (-1, 0, 1)], axis=0)
    ends = jnp.concatenate(
        [turned[sz][part] for sz in (-1, 0, 1) for part in (slice(0, C), slice(LANES - C, LANES))],
        axis=0,
    )
    blocks = lane_block()
    sums = {}
    for sy in (-1, 0, 1):
        rows = pl.ds((1 + sy) * NZ, OWN)
        main = dot(tall, cells[field, rows, :])
        edge = dot(ends, rim[rows, :])
        for n, sz in enumerate((-1, 0, 1)):
            for sx in (-1, 0, 1):
                halves = []
                for tile in range(2):
                    value = None
                    for b in range(4):
                        a = 4 * tile + b - sx
                        if 0 <= a < SIDE:
                            top = n * LANES + a * C
                            term = main[top : top + C, tile * 128 : tile * 128 + 128]
                        else:
                            term = jnp.zeros((C, 128), F32)
                        value = term if value is None else jnp.where(blocks >= b, term, value)
                    halves.append(value)
                total = halves[0] + halves[1]
                if sx == -1:
                    total = total + jnp.where(blocks == 2 * field, edge[n * 64 : n * 64 + C], 0.0)
                if sx == 1:
                    total = total + jnp.where(
                        blocks == 2 * field + 1, edge[n * 64 + C : n * 64 + 64], 0.0
                    )
                sums[sx, sy, sz] = total
    return sums


def fold_four(a, b, c, d):
    blocks = lane_block()
    low = blocks < 2
    middle = (blocks == 1) | (blocks == 2)
    even = (blocks == 0) | (blocks == 2)
    ac = jnp.where(low, a, c) + pltpu.roll(jnp.where(low, c, a), 64, 1)
    bd = jnp.where(middle, b, d) + pltpu.roll(jnp.where(middle, d, b), 64, 1)
    return jnp.where(even, ac, bd) + pltpu.roll(jnp.where(even, bd, ac), 96, 1)


def kernel(
    n_gx, n_gy, factor,
    list_any, f_any, g_any, w1_any, w2_any,
    block_ref, back_ref, one_ref, two_ref,
    turned_a, cells_a, side_a, corner_a, rim_a,
    turned_b, cells_b, side_b, corner_b, rim_b,
    quad, band, rim_in, rim_out,
    packed, gathered, column, total,
    list_ref, fields_in, weights_in,
    list_sem, f_sem, g_sem, w1_sem, w2_sem,
    halo_send_a, halo_recv_a, halo_send_b, halo_recv_b,
    part_send, part_recv, line_send, line_recv, full_send, full_recv, hails,
):
    gx, gy = lax.axis_index("gx"), lax.axis_index("gy")
    n_line = n_gx // X_HI
    n_plane = X_HI * n_gy
    x_hi = jnp.where(gx >= n_line, 1, 0)
    line = gx - x_hi * n_line
    rank = x_hi * n_gy + gy
    share = PACKED // n_plane
    n_seats = n_plane // 2
    n_busy = -(-7 * C // share)
    seat = rank // 2
    half = rank - 2 * seat
    busy = seat < n_busy

    def wrapped(value, count):
        value = jnp.where(value >= count, value - count, value)
        return jnp.where(value < 0, value + count, value)

    def beside(dx, dy):
        return (wrapped(gx + dx, n_gx), wrapped(gy + dy, n_gy))

    def in_plane(other):
        hi = jnp.where(other >= n_gy, 1, 0)
        return (hi * n_line + line, other - hi * n_gy)

    def in_line(other):
        return (x_hi * n_line + other, gy)

    n_x, n_y = X_HI * X_LO, n_gy // (X_LO * CORES)
    y = gy // (X_LO * CORES)
    x = x_hi * X_LO + gy // CORES - y * X_LO

    def hops(offset, count):
        return min(offset, count - offset)

    chips = [(dy, dx) for dy in range(n_y) for dx in range(n_x)]
    chips.sort(key=lambda chip: -hops(chip[0], n_y) - hops(chip[1], n_x))
    steps = sorted(range(1, n_line), key=lambda d: -hops(d, n_line))

    def seat_at(dy, dx):
        other_y, other_x = wrapped(y + dy, n_y), wrapped(x + dx, n_x)
        hi = jnp.where(other_x >= X_LO, 1, 0)
        return hi * (n_seats - n_seats // X_HI) + other_y * X_LO + other_x - hi * X_LO

    barrier = pltpu.get_barrier_semaphore()
    around = [(dx, dy) for dx in (-1, 0, 1) for dy in (-1, 0, 1) if (dx, dy) != (0, 0)]
    far_chips = [chip for chip in chips if hops(chip[0], n_y) + hops(chip[1], n_x) > REACH]
    far_line = [d for d in steps if hops(d, n_line) > REACH]
    greeted = [in_line(wrapped(line + d, n_line)) for d in steps if d not in far_line]
    for chip in chips:
        if chip not in far_chips and chip != (0, 0):
            greeted += [in_plane(2 * seat_at(*chip) + core) for core in range(CORES)]
    greeted.append(in_plane(2 * seat + 1 - half))
    greeted += [beside(dx, dy) for dx, dy in around]
    for target in greeted:
        pl.semaphore_signal(barrier, inc=1, device_id=target, device_id_type=MESH)

    hailed = [[], []]
    if far_chips:
        hailed[0].append(in_plane(2 * seat_at(n_y - 1, 0) + half))
    if far_line:
        hailed[0] += [in_line(wrapped(line + d, n_line)) for d in (REACH, -REACH)]
        rest = n_line // 2 - 2 * REACH
        hailed[1] += [in_line(wrapped(line + d, n_line)) for d in (rest, -rest)]

    def hail(n):
        for target in hailed[n]:
            pl.semaphore_signal(hails.at[n], inc=1, device_id=target, device_id_type=MESH)

    def await_hail(n):
        if hailed[n]:
            pl.semaphore_wait(hails.at[n], len(hailed[n]))

    loads = [
        pltpu.make_async_copy(src, dst, sem)
        for src, dst, sem in (
            (list_any, list_ref, list_sem),
            (f_any, fields_in.at[0], f_sem),
            (g_any, fields_in.at[1], g_sem),
            (w1_any, weights_in.at[0], w1_sem),
            (w2_any, weights_in.at[1], w2_sem),
        )
    ]
    for load in loads:
        load.start()

    loads[0].wait()
    hits = []
    for brick in range(BRICKS):
        count = jnp.int32(0)
        for slot in range(BRICKS):
            count = count + jnp.where(list_ref[0, 0, slot] == brick, 1, 0)
        hits.append(count.astype(F32))
    occupied = jnp.concatenate(
        [jnp.full((8, LANES), hit, F32) for hit in hits] * SIDE, axis=0
    )
    brick_of = lax.rem(lax.broadcasted_iota(jnp.int32, (8, OWN), 1), NZ) // 8
    across = jnp.zeros((8, OWN), F32)
    for brick in range(BRICKS):
        across = across + jnp.where(brick_of == brick, hits[brick], 0.0)
    across = jnp.concatenate([across] * (LANES // 8), axis=0)

    row = lax.broadcasted_iota(jnp.int32, (LANES, LANES), 0)
    col = lax.broadcasted_iota(jnp.int32, (LANES, LANES), 1)
    order = jnp.where(col == (row % C) * SIDE + row // C, 1.0, 0.0).astype(BF16)
    reorder = jnp.where(row == (col % C) * SIDE + col // C, 1.0, 0.0).astype(BF16)
    for field in range(2):
        loads[1 + field].wait()
        value = (dot(order, fields_in[field]) * across).astype(BF16)
        turned_a[field] = value
        cells_a[field, pl.ds(NZ, OWN), :] = value.T

    pl.semaphore_wait(barrier, len(greeted))

    def exchange(turned, cells, side, corner, send, recv):
        low, high = pl.ds(0, C), pl.ds(LANES - C, C)
        every, head, tail = pl.ds(0, OWN), pl.ds(0, 128), pl.ds(OWN - 128, 128)

        def strip(rows, lanes):
            return turned.at[:, rows, lanes]

        def slab(y):
            return cells.at[:, pl.ds((y + 1) * NZ, NZ), :]

        def remote_copy(src, dst, group, dx, dy):
            return pltpu.make_async_remote_copy(
                src_ref=src,
                dst_ref=dst,
                send_sem=send.at[group],
                recv_sem=recv.at[group],
                device_id=beside(dx, dy),
                device_id_type=MESH,
            )

        @pl.when(gx < n_gx - 1)
        def _():
            remote_copy(strip(high, tail), corner.at[0], 1, 1, 1).start()
            remote_copy(strip(high, head), corner.at[2], 1, 1, -1).start()
            remote_copy(strip(high, every), side.at[0], 1, 1, 0).start()

        @pl.when(gx > 0)
        def _():
            remote_copy(strip(low, tail), corner.at[1], 2, -1, 1).start()
            remote_copy(strip(low, head), corner.at[3], 2, -1, -1).start()
            remote_copy(strip(low, every), side.at[1], 2, -1, 0).start()

        remote_copy(slab(SIDE - 1), slab(-1), 0, 0, 1).start()
        remote_copy(slab(0), slab(SIDE), 0, 0, -1).start()

        slabs = turned.at[0, pl.ds(0, 2 * NZ * 2), pl.ds(0, 256)]
        strips = turned.at[0, pl.ds(0, 160), pl.ds(0, 256)]

        def wait_recv():
            remote_copy(slabs, slabs, 0, 0, 1).wait_recv()

            @pl.when(gx > 0)
            def _():
                remote_copy(strips, strips, 1, 1, 0).wait_recv()

            @pl.when(gx < n_gx - 1)
            def _():
                remote_copy(strips, strips, 2, 1, 0).wait_recv()

        def wait_send():
            remote_copy(slabs, slabs, 0, 0, 1).wait_send()

            @pl.when(gx < n_gx - 1)
            def _():
                remote_copy(strips, strips, 1, 1, 0).wait_send()

            @pl.when(gx > 0)
            def _():
                remote_copy(strips, strips, 2, 1, 0).wait_send()

        return wait_recv, wait_send

    def place_rims(copies, cells, side, corner, rim):
        copies[0]()
        first_y, last_y = gy > 0, gy < n_gy - 1
        for rows, keep in ((pl.ds(0, NZ), first_y), (pl.ds(ALL - NZ, NZ), last_y)):
            for field in range(2):
                kept = jnp.where(keep, cells[field, rows, :].astype(F32), 0.0)
                cells[field, rows, :] = kept.astype(BF16)
        odd = lax.rem(lane_block((1, 128)), 2)
        inside = jnp.where(odd == 1, jnp.where(gx < n_gx - 1, 1, 0), jnp.where(gx > 0, 1, 0))

        def turn(left, right, keep):
            parts = [left[0], right[0], left[1], right[1]]
            value = jnp.concatenate(parts, axis=0).T.astype(F32)
            return jnp.where(inside * jnp.where(keep, 1, 0) > 0, value, 0.0).astype(BF16)

        rim[pl.ds(NZ, OWN), :] = turn(side[0], side[1], True)
        rim[pl.ds(0, NZ), :] = turn(corner[0], corner[1], first_y)[128 - NZ :]
        rim[pl.ds(ALL - NZ, NZ), :] = turn(corner[2], corner[3], last_y)[:NZ]

    copies_a = exchange(turned_a, cells_a, side_a, corner_a, halo_send_a, halo_recv_a)
    hail(0)
    for w in range(2):
        loads[3 + w].wait()
        widen_weights(weights_in, quad, w)
    build_bands(quad, band, rim_in, rim_out)
    place_rims(copies_a, cells_a, side_a, corner_a, rim_a)

    pre_one = conv_forward(cells_a, rim_a, band, rim_in, 0) * occupied
    sigma = jax.nn.sigmoid(pre_one)
    hidden = (pre_one * sigma).astype(BF16)
    slope = occupied * sigma * (1.0 + pre_one * (1.0 - sigma))
    delta = (conv_backward(cells_a, rim_a, band, rim_out, 1) * slope).astype(BF16)
    for field, value in enumerate((hidden, delta)):
        cells_b[field, pl.ds(NZ, OWN), :] = value
        turned_b[field] = value.T

    def share_of(ref, other):
        other_seat = other // 2
        top = (other - 2 * other_seat) * (PACKED // 2) + other_seat * share
        return ref.at[pl.ds(pl.multiple_of(top, share), share), :]

    def remote(src, dst, send, recv, device):
        return pltpu.make_async_remote_copy(
            src_ref=src,
            dst_ref=dst,
            send_sem=send,
            recv_sem=recv,
            device_id=device,
            device_id_type=MESH,
        )

    def part_copy(target):
        src, dst = share_of(packed, target), gathered.at[rank]
        return remote(src, dst, part_send, part_recv, in_plane(target))

    def line_copy(target):
        src, dst = column.at[line], column.at[line]
        return remote(src, dst, line_send, line_recv, in_line(target))

    def full_copy(target):
        src, dst = share_of(total, rank), share_of(total, rank)
        return remote(src, dst, full_send, full_recv, in_plane(target))

    def start_parts(which):
        for chip in chips:
            other = seat_at(*chip)

            @pl.when((other < n_busy) & (2 * other + which != rank))
            def _():
                part_copy(2 * other + which).start()

    def start_line():
        for d in steps:
            line_copy(wrapped(line + d, n_line)).start()

    def start_full():
        for chip in chips:
            other = 2 * seat_at(*chip)
            for core in range(CORES):
                if chip == (0, 0):
                    continue
                full_copy(other + core).start()
        full_copy(2 * seat + 1 - half).start()

    def whole(ref, count, send, recv):
        part = ref.at[pl.ds(0, count)]
        return remote(part, part, send, recv, beside(1, 0))

    part_all = whole(gathered, n_plane - 1, part_send, part_recv)
    line_all = whole(column, n_line - 1, line_send, line_recv)

    def when_busy(busy_act, idle_act):
        pl.when(busy)(busy_act)
        if n_busy < n_seats:
            pl.when(jnp.logical_not(busy))(idle_act)

    def nothing():
        pass

    def wait_parts_sent():
        sent = 2 * n_busy
        when_busy(
            whole(gathered, sent - 1, part_send, part_recv).wait_send,
            whole(gathered, sent, part_send, part_recv).wait_send,
        )

    def wait_full():
        landed = 2 * n_busy * share
        when_busy(
            whole(total, landed - share, full_send, full_recv).wait_recv,
            whole(total, landed, full_send, full_recv).wait_recv,
        )

    def wait_full_sent():
        when_busy(
            whole(total, (n_plane - 1) * share, full_send, full_recv).wait_send, nothing
        )

    def summed(ref, count):
        value = ref[0].astype(F32)
        for n in range(1, count):
            value = value + ref[n].astype(F32)
        return value

    copies_b = exchange(turned_b, cells_b, side_b, corner_b, halo_send_b, halo_recv_b)
    offsets = [(kx, ky, kz) for kx in (-1, 0, 1) for ky in (-1, 0, 1) for kz in (-1, 0, 1)]
    for which, own, field, sign in ((0, hidden, 1, -1), (1, delta, 0, 1)):
        sums = kernel_sums(own, cells_a, rim_a, field)
        parts = [sums[tuple(sign * o for o in offset)] for offset in offsets]
        parts.append(jnp.zeros((C, 128), F32))
        top = which * (PACKED // 2)
        for n, first in enumerate(range(0, 28, 4)):
            packed[pl.ds(top + n * C, C), :] = fold_four(*parts[first : first + 4])
        packed[pl.ds(top + 7 * C, C), :] = jnp.zeros((C, 128), F32)
        if which == 0:
            await_hail(0)
            hail(1)
        start_parts(which)


    await_hail(1)

    @pl.when(busy)
    def _():
        gathered[rank] = share_of(packed, rank)[...]
        part_all.wait_recv()
        column[line] = summed(gathered, n_plane).astype(BF16)
        start_line()

    place_rims(copies_b, cells_b, side_b, corner_b, rim_b)
    pre_two = conv_forward(cells_b, rim_b, band, rim_in, 1) * occupied
    middle = pl.ds(NZ, OWN)
    block_out = (cells_a[0, middle, :].astype(F32) + pre_two).astype(BF16)
    block_ref[...] = dot(reorder, block_out, ((1,), (1,))).astype(BF16)
    back = conv_backward(cells_b, rim_b, band, rim_out, 0) * occupied
    grad_features = (cells_a[1, middle, :].astype(F32) + back).astype(BF16)
    back_ref[...] = dot(reorder, grad_features, ((1,), (1,))).astype(BF16)

    @pl.when(busy)
    def _():
        line_all.wait_recv()
        share_of(total, rank)[...] = summed(column, n_line).astype(BF16)
        start_full()

    copies_a[1]()
    copies_b[1]()
    wait_parts_sent()
    pl.when(busy)(line_all.wait_send)
    wait_full()

    for n, first in enumerate(range(0, 27, 4)):
        count = min(4, 27 - first)
        one_ref[pl.ds(first * C, count * C), :] = (
            total[pl.ds(PACKED // 2 + n * C, C), :].astype(F32).T[: count * C] * factor
        )
        group = total[pl.ds(n * C, C), :].astype(F32) * factor
        for k in range(count):
            two_ref[pl.ds((first + k) * C, C), :] = group[:, k * C : (k + 1) * C]
    wait_full_sent()


def deliver(*refs):
    results, outs, sems = refs[:4], refs[4:8], refs[8]
    copies = []
    for n, (result, out) in enumerate(zip(results, outs)):
        rows = result.shape[0] // PIECES
        for piece in range(PIECES):
            part = pl.ds(piece * rows, rows)
            sem = sems.at[n, piece]
            copies.append(pltpu.make_async_copy(result.at[part], out.at[part], sem))
    for copy in copies:
        copy.start()
    for copy in copies:
        copy.wait()


def per_device(features, brick_list, weight_one, weight_two, cotangent):
    n_gx, n_gy = lax.axis_size("gx"), lax.axis_size("gy")
    n_line, n_plane = n_gx // X_HI, X_HI * n_gy
    share = PACKED // n_plane
    factor = float(n_gx * SIDE * n_gy * SIDE * NZ) ** (-0.5)
    vmem = pl.BlockSpec(memory_space=pltpu.VMEM)
    halo = [
        pltpu.VMEM((2, LANES, OWN), BF16),
        pltpu.VMEM((2, ALL, LANES), BF16),
        pltpu.VMEM((2, 2, C, OWN), BF16),
        pltpu.VMEM((4, 2, C, 128), BF16),
        pltpu.VMEM((ALL, 128), BF16),
    ]
    out_shape = (
        jax.ShapeDtypeStruct((LANES, OWN), BF16),
        jax.ShapeDtypeStruct((LANES, OWN), BF16),
        jax.ShapeDtypeStruct((27 * C, C), F32),
        jax.ShapeDtypeStruct((27 * C, C), F32),
    )
    arguments = (
        brick_list,
        features.reshape(LANES, OWN),
        cotangent.reshape(LANES, OWN),
        weight_one.reshape(27 * C, C),
        weight_two.reshape(27 * C, C),
    )
    results = pl.pallas_call(
        functools.partial(kernel, n_gx, n_gy, factor),
        out_shape=tuple(pltpu.VMEM(result.shape, result.dtype) for result in out_shape),
        in_specs=[pl.BlockSpec(memory_space=pltpu.HBM)] * 5,
        out_specs=[vmem] * 4,
        scratch_shapes=halo
        + halo
        + [
            pltpu.VMEM((2, 27, C, 128), BF16),
            pltpu.VMEM((2, 3, LANES, 3 * LANES), BF16),
            pltpu.VMEM((2, 3, 128, 3 * LANES), BF16),
            pltpu.VMEM((2, 3, LANES, 3 * 128), BF16),
            pltpu.VMEM((PACKED, 128), F32),
            pltpu.VMEM((n_plane, share, 128), F32),
            pltpu.VMEM((n_line, share, 128), BF16),
            pltpu.VMEM((PACKED, 128), BF16),
        ]
        + [
            pltpu.SMEM((1, 1, BRICKS), jnp.int32),
            pltpu.VMEM((2, LANES, OWN), BF16),
            pltpu.VMEM((2, 27 * C, C), BF16),
        ]
        + [pltpu.SemaphoreType.DMA] * 5
        + [pltpu.SemaphoreType.DMA((3,))] * 4
        + [pltpu.SemaphoreType.DMA] * 6
        + [pltpu.SemaphoreType.REGULAR((2,))],
        compiler_params=pltpu.CompilerParams(
            collective_id=0, has_side_effects=True, vmem_limit_bytes=40 * 1024 * 1024
        ),
    )(*[pltpu.with_memory_space_constraint(value, pltpu.HBM) for value in arguments])
    block_out, grad_features, one, two = pl.pallas_call(
        deliver,
        out_shape=out_shape,
        in_specs=[vmem] * 4,
        out_specs=[pl.BlockSpec(memory_space=pl.ANY)] * 4,
        scratch_shapes=[pltpu.SemaphoreType.DMA((4, PIECES))],
        compiler_params=pltpu.CompilerParams(vmem_limit_bytes=4 * 1024 * 1024),
    )(*[pltpu.with_memory_space_constraint(value, pltpu.VMEM) for value in results])
    flat = (C, SIDE, OWN)
    cube = (3, 3, 3, C, C)
    return block_out.reshape(flat), grad_features.reshape(flat), one.reshape(cube), two.reshape(cube)


def solution(mesh):
    return jax.shard_map(
        per_device,
        mesh=mesh,
        in_specs=(P(None, "gx", "gy"), P("gx", "gy", None), P(), P(), P(None, "gx", "gy")),
        out_specs=(P(None, "gx", "gy"), P(None, "gx", "gy"), P(), P()),
        check_vma=False,
    )
```

```python
import functools

import jax
import jax.numpy as jnp
from jax import lax
from jax.experimental import pallas as pl
from jax.experimental.pallas import tpu as pltpu
from jax.sharding import PartitionSpec as P

C = 32
SIDE = 8
NZ = 48
BRICKS = 6
LANES = SIDE * C
OWN = SIDE * NZ
ALL = OWN + 2 * NZ
PACKED = 512
PIECES = 4
X_HI = 2
REACH = 3
X_LO = 2
CORES = 2
MESH = pl.DeviceIdType.MESH
F32 = jnp.float32
BF16 = jnp.bfloat16


def dot(a, b, contract=((1,), (0,))):
    return lax.dot_general(a, b, (contract, ((), ())), preferred_element_type=F32)


def rows_mask(zero_at):
    z = lax.broadcasted_iota(jnp.int32, (NZ, LANES), 0)
    return jnp.concatenate([jnp.where(z == zero_at, 0.0, 1.0).astype(F32)] * SIDE, axis=0)


def from_below(value):
    return pltpu.roll(value, 1, 0) * rows_mask(0)


def from_above(value):
    return pltpu.roll(value, OWN - 1, 0) * rows_mask(NZ - 1)


def at(kx, ky, kz):
    return kx * 9 + ky * 3 + kz


def lane_block(shape=(C, 128)):
    return lax.broadcasted_iota(jnp.int32, shape, 1) // C


def widen_weights(w_ref, quad, which):
    lane = lax.broadcasted_iota(jnp.int32, (C, 128), 1)
    row = lax.broadcasted_iota(jnp.int32, (C, 128), 0)
    repeat = jnp.where(lane % C == row, 1.0, 0.0).astype(BF16)
    quad[which] = dot(w_ref[which], repeat).astype(BF16).reshape(27, C, 128)


def build_bands(quad, band, rim_in, rim_out):
    blocks = lane_block()
    masks = [jnp.where(blocks == b, 1.0, 0.0).astype(BF16) for b in range(4)]
    zero = jnp.zeros((C, 128), BF16)

    def step(i, carry):
        w, ky = i // 3, lax.rem(i, 3)
        rim_in[w, ky] = jnp.zeros((128, 3 * LANES), BF16)
        rim_out[w, ky] = jnp.zeros((LANES, 3 * 128), BF16)
        for kz in range(3):
            parts = [quad[w, at(kx, ky, kz)] for kx in range(3)]
            for xi in range(SIDE):
                for tile in range(2):
                    value = None
                    for kx in range(3):
                        xo = xi + 1 - kx - 4 * tile
                        if 0 <= xo < 4:
                            term = parts[kx] * masks[xo]
                            value = term if value is None else value + term
                    lanes = pl.ds(kz * LANES + tile * 128, 128)
                    band[w, ky, pl.ds(xi * C, C), lanes] = zero if value is None else value
            rim_in[w, ky, pl.ds(0, C), pl.ds(kz * LANES, 128)] = parts[0] * masks[0]
            rim_in[w, ky, pl.ds(C, C), pl.ds(kz * LANES + 128, 128)] = parts[2] * masks[3]
            rim_out[w, ky, pl.ds(0, C), pl.ds(kz * 128, 128)] = parts[2] * masks[2]
            rim_out[w, ky, pl.ds(LANES - C, C), pl.ds(kz * 128, 128)] = parts[0] * masks[3]
        return carry

    lax.fori_loop(0, 6, step, 0)


def shifted_rows(cells, rim, field):
    parts = [cells[field, pl.ds(ky * NZ, OWN), :] for ky in range(3)]
    return jnp.concatenate(parts + [rim[pl.ds(ky * NZ, OWN), :] for ky in range(3)], axis=1)


def conv_forward(cells, rim, band, rim_in, w):
    lhs = shifted_rows(cells, rim, 0)
    terms = []
    for kz in range(3):
        lanes = pl.ds(kz * LANES, LANES)
        rhs = jnp.concatenate(
            [band[w, ky, :, lanes] for ky in range(3)]
            + [rim_in[w, ky, :, lanes] for ky in range(3)],
            axis=0,
        )
        terms.append(dot(lhs, rhs))
    return terms[1] + from_below(terms[0]) + from_above(terms[2])


def conv_backward(cells, rim, band, rim_out, w):
    lhs = shifted_rows(cells, rim, 1)
    terms = []
    for kz in range(3):
        back = 2 - kz
        rhs = jnp.concatenate(
            [band[w, 2 - ky, :, pl.ds(back * LANES, LANES)] for ky in range(3)]
            + [rim_out[w, 2 - ky, :, pl.ds(back * 128, 128)] for ky in range(3)],
            axis=1,
        )
        terms.append(dot(lhs, rhs, ((1,), (1,))))
    return terms[1] + from_below(terms[0]) + from_above(terms[2])


def kernel_sums(own, cells, rim, field):
    wide = own.astype(F32)
    turned = {
        -1: from_above(wide).astype(BF16).T,
        0: own.T,
        1: from_below(wide).astype(BF16).T,
    }
    tall = jnp.concatenate([turned[sz] for sz in (-1, 0, 1)], axis=0)
    ends = jnp.concatenate(
        [turned[sz][part] for sz in (-1, 0, 1) for part in (slice(0, C), slice(LANES - C, LANES))],
        axis=0,
    )
    blocks = lane_block()
    sums = {}
    shifts = [pl.ds(shift * NZ, OWN) for shift in range(3)]
    mains = dot(tall, jnp.concatenate([cells[field, rows, :] for rows in shifts], axis=1))
    edges = dot(ends, jnp.concatenate([rim[rows, :] for rows in shifts], axis=1))
    for sy in (-1, 0, 1):
        main = mains[:, (1 + sy) * LANES : (2 + sy) * LANES]
        edge = edges[:, (1 + sy) * 128 : (2 + sy) * 128]
        for n, sz in enumerate((-1, 0, 1)):
            for sx in (-1, 0, 1):
                halves = []
                for tile in range(2):
                    value = None
                    for b in range(4):
                        a = 4 * tile + b - sx
                        if 0 <= a < SIDE:
                            top = n * LANES + a * C
                            term = main[top : top + C, tile * 128 : tile * 128 + 128]
                        else:
                            term = jnp.zeros((C, 128), F32)
                        value = term if value is None else jnp.where(blocks >= b, term, value)
                    halves.append(value)
                total = halves[0] + halves[1]
                if sx == -1:
                    total = total + jnp.where(blocks == 2 * field, edge[n * 64 : n * 64 + C], 0.0)
                if sx == 1:
                    total = total + jnp.where(
                        blocks == 2 * field + 1, edge[n * 64 + C : n * 64 + 64], 0.0
                    )
                sums[sx, sy, sz] = total
    return sums


def fold_four(a, b, c, d):
    blocks = lane_block()
    low = blocks < 2
    middle = (blocks == 1) | (blocks == 2)
    even = (blocks == 0) | (blocks == 2)
    ac = jnp.where(low, a, c) + pltpu.roll(jnp.where(low, c, a), 64, 1)
    bd = jnp.where(middle, b, d) + pltpu.roll(jnp.where(middle, d, b), 64, 1)
    return jnp.where(even, ac, bd) + pltpu.roll(jnp.where(even, bd, ac), 96, 1)


def kernel(
    n_gx, n_gy, factor,
    list_any, f_any, g_any, w1_any, w2_any,
    block_ref, back_ref, one_ref, two_ref,
    turned_a, cells_a, side_a, corner_a, rim_a,
    turned_b, cells_b, side_b, corner_b, rim_b,
    quad, band, rim_in, rim_out,
    packed, gathered, column, total,
    list_ref, fields_in, weights_in,
    list_sem, f_sem, g_sem, w1_sem, w2_sem,
    halo_send_a, halo_recv_a, halo_send_b, halo_recv_b,
    part_send, part_recv, line_send, line_recv, full_send, full_recv, hails,
):
    gx, gy = lax.axis_index("gx"), lax.axis_index("gy")
    n_line = n_gx // X_HI
    n_plane = X_HI * n_gy
    x_hi = jnp.where(gx >= n_line, 1, 0)
    line = gx - x_hi * n_line
    rank = x_hi * n_gy + gy
    share = PACKED // n_plane
    n_seats = n_plane // 2
    n_busy = -(-7 * C // share)
    seat = rank // 2
    half = rank - 2 * seat
    busy = seat < n_busy

    def wrapped(value, count):
        value = jnp.where(value >= count, value - count, value)
        return jnp.where(value < 0, value + count, value)

    def beside(dx, dy):
        return (wrapped(gx + dx, n_gx), wrapped(gy + dy, n_gy))

    def in_plane(other):
        hi = jnp.where(other >= n_gy, 1, 0)
        return (hi * n_line + line, other - hi * n_gy)

    def in_line(other):
        return (x_hi * n_line + other, gy)

    n_x, n_y = X_HI * X_LO, n_gy // (X_LO * CORES)
    y = gy // (X_LO * CORES)
    x = x_hi * X_LO + gy // CORES - y * X_LO

    def hops(offset, count):
        return min(offset, count - offset)

    chips = [(dy, dx) for dy in range(n_y) for dx in range(n_x)]
    chips.sort(key=lambda chip: -hops(chip[0], n_y) - hops(chip[1], n_x))
    steps = sorted(range(1, n_line), key=lambda d: -hops(d, n_line))

    def seat_at(dy, dx):
        other_y, other_x = wrapped(y + dy, n_y), wrapped(x + dx, n_x)
        hi = jnp.where(other_x >= X_LO, 1, 0)
        return hi * (n_seats - n_seats // X_HI) + other_y * X_LO + other_x - hi * X_LO

    barrier = pltpu.get_barrier_semaphore()
    around = [(dx, dy) for dx in (-1, 0, 1) for dy in (-1, 0, 1) if (dx, dy) != (0, 0)]
    far_chips = [chip for chip in chips if hops(chip[0], n_y) + hops(chip[1], n_x) > REACH]
    far_line = [d for d in steps if hops(d, n_line) > REACH]
    greeted = [in_line(wrapped(line + d, n_line)) for d in steps if d not in far_line]
    for chip in chips:
        if chip not in far_chips and chip != (0, 0):
            greeted += [in_plane(2 * seat_at(*chip) + core) for core in range(CORES)]
    greeted.append(in_plane(2 * seat + 1 - half))
    greeted += [beside(dx, dy) for dx, dy in around]
    for target in greeted:
        pl.semaphore_signal(barrier, inc=1, device_id=target, device_id_type=MESH)

    hailed = [[], []]
    if far_chips:
        hailed[0].append(in_plane(2 * seat_at(n_y - 1, 0) + half))
    if far_line:
        hailed[0] += [in_line(wrapped(line + d, n_line)) for d in (REACH, -REACH)]
        rest = n_line // 2 - 2 * REACH
        hailed[1] += [in_line(wrapped(line + d, n_line)) for d in (rest, -rest)]

    def hail(n):
        for target in hailed[n]:
            pl.semaphore_signal(hails.at[n], inc=1, device_id=target, device_id_type=MESH)

    def await_hail(n):
        if hailed[n]:
            pl.semaphore_wait(hails.at[n], len(hailed[n]))

    loads = [
        pltpu.make_async_copy(src, dst, sem)
        for src, dst, sem in (
            (list_any, list_ref, list_sem),
            (f_any, fields_in.at[0], f_sem),
            (g_any, fields_in.at[1], g_sem),
            (w1_any, weights_in.at[0], w1_sem),
            (w2_any, weights_in.at[1], w2_sem),
        )
    ]
    for load in loads:
        load.start()

    loads[0].wait()
    hits = []
    for brick in range(BRICKS):
        count = jnp.int32(0)
        for slot in range(BRICKS):
            count = count + jnp.where(list_ref[0, 0, slot] == brick, 1, 0)
        hits.append(count.astype(F32))
    occupied = jnp.concatenate(
        [jnp.full((8, LANES), hit, F32) for hit in hits] * SIDE, axis=0
    )
    brick_of = lax.rem(lax.broadcasted_iota(jnp.int32, (8, OWN), 1), NZ) // 8
    across = jnp.zeros((8, OWN), F32)
    for brick in range(BRICKS):
        across = across + jnp.where(brick_of == brick, hits[brick], 0.0)
    across = jnp.concatenate([across] * (LANES // 8), axis=0)

    row = lax.broadcasted_iota(jnp.int32, (LANES, LANES), 0)
    col = lax.broadcasted_iota(jnp.int32, (LANES, LANES), 1)
    order = jnp.where(col == (row % C) * SIDE + row // C, 1.0, 0.0).astype(BF16)
    reorder = jnp.where(row == (col % C) * SIDE + col // C, 1.0, 0.0).astype(BF16)
    for field in range(2):
        loads[1 + field].wait()
        value = (dot(order, fields_in[field]) * across).astype(BF16)
        turned_a[field] = value
        cells_a[field, pl.ds(NZ, OWN), :] = value.T

    pl.semaphore_wait(barrier, len(greeted))

    def exchange(turned, cells, side, corner, send, recv):
        low, high = pl.ds(0, C), pl.ds(LANES - C, C)
        every, head, tail = pl.ds(0, OWN), pl.ds(0, 128), pl.ds(OWN - 128, 128)

        def strip(rows, lanes):
            return turned.at[:, rows, lanes]

        def slab(y):
            return cells.at[:, pl.ds((y + 1) * NZ, NZ), :]

        def remote_copy(src, dst, group, dx, dy):
            return pltpu.make_async_remote_copy(
                src_ref=src,
                dst_ref=dst,
                send_sem=send.at[group],
                recv_sem=recv.at[group],
                device_id=beside(dx, dy),
                device_id_type=MESH,
            )

        @pl.when(gx < n_gx - 1)
        def _():
            remote_copy(strip(high, tail), corner.at[0], 1, 1, 1).start()
            remote_copy(strip(high, head), corner.at[2], 1, 1, -1).start()
            remote_copy(strip(high, every), side.at[0], 1, 1, 0).start()

        @pl.when(gx > 0)
        def _():
            remote_copy(strip(low, tail), corner.at[1], 2, -1, 1).start()
            remote_copy(strip(low, head), corner.at[3], 2, -1, -1).start()
            remote_copy(strip(low, every), side.at[1], 2, -1, 0).start()

        remote_copy(slab(SIDE - 1), slab(-1), 0, 0, 1).start()
        remote_copy(slab(0), slab(SIDE), 0, 0, -1).start()

        slabs = turned.at[0, pl.ds(0, 2 * NZ * 2), pl.ds(0, 256)]
        strips = turned.at[0, pl.ds(0, 160), pl.ds(0, 256)]

        def wait_recv():
            remote_copy(slabs, slabs, 0, 0, 1).wait_recv()

            @pl.when(gx > 0)
            def _():
                remote_copy(strips, strips, 1, 1, 0).wait_recv()

            @pl.when(gx < n_gx - 1)
            def _():
                remote_copy(strips, strips, 2, 1, 0).wait_recv()

        def wait_send():
            remote_copy(slabs, slabs, 0, 0, 1).wait_send()

            @pl.when(gx < n_gx - 1)
            def _():
                remote_copy(strips, strips, 1, 1, 0).wait_send()

            @pl.when(gx > 0)
            def _():
                remote_copy(strips, strips, 2, 1, 0).wait_send()

        return wait_recv, wait_send

    def place_rims(copies, cells, side, corner, rim):
        copies[0]()
        first_y, last_y = gy > 0, gy < n_gy - 1
        for rows, keep in ((pl.ds(0, NZ), first_y), (pl.ds(ALL - NZ, NZ), last_y)):
            for field in range(2):
                kept = jnp.where(keep, cells[field, rows, :].astype(F32), 0.0)
                cells[field, rows, :] = kept.astype(BF16)
        odd = lax.rem(lane_block((1, 128)), 2)
        inside = jnp.where(odd == 1, jnp.where(gx < n_gx - 1, 1, 0), jnp.where(gx > 0, 1, 0))

        def turn(left, right, keep):
            parts = [left[0], right[0], left[1], right[1]]
            value = jnp.concatenate(parts, axis=0).T.astype(F32)
            return jnp.where(inside * jnp.where(keep, 1, 0) > 0, value, 0.0).astype(BF16)

        rim[pl.ds(NZ, OWN), :] = turn(side[0], side[1], True)
        rim[pl.ds(0, NZ), :] = turn(corner[0], corner[1], first_y)[128 - NZ :]
        rim[pl.ds(ALL - NZ, NZ), :] = turn(corner[2], corner[3], last_y)[:NZ]

    copies_a = exchange(turned_a, cells_a, side_a, corner_a, halo_send_a, halo_recv_a)
    hail(0)
    for w in range(2):
        loads[3 + w].wait()
        widen_weights(weights_in, quad, w)
    build_bands(quad, band, rim_in, rim_out)
    place_rims(copies_a, cells_a, side_a, corner_a, rim_a)

    pre_one = conv_forward(cells_a, rim_a, band, rim_in, 0) * occupied
    sigma = jax.nn.sigmoid(pre_one)
    hidden = (pre_one * sigma).astype(BF16)
    slope = occupied * sigma * (1.0 + pre_one * (1.0 - sigma))
    delta = (conv_backward(cells_a, rim_a, band, rim_out, 1) * slope).astype(BF16)
    for field, value in enumerate((hidden, delta)):
        cells_b[field, pl.ds(NZ, OWN), :] = value
        turned_b[field] = value.T

    def share_of(ref, other):
        other_seat = other // 2
        top = (other - 2 * other_seat) * (PACKED // 2) + other_seat * share
        return ref.at[pl.ds(pl.multiple_of(top, share), share), :]

    def remote(src, dst, send, recv, device):
        return pltpu.make_async_remote_copy(
            src_ref=src,
            dst_ref=dst,
            send_sem=send,
            recv_sem=recv,
            device_id=device,
            device_id_type=MESH,
        )

    def part_copy(target):
        src, dst = share_of(packed, target), gathered.at[rank]
        return remote(src, dst, part_send, part_recv, in_plane(target))

    def line_copy(target):
        src, dst = column.at[line], column.at[line]
        return remote(src, dst, line_send, line_recv, in_line(target))

    def full_copy(target):
        src, dst = share_of(total, rank), share_of(total, rank)
        return remote(src, dst, full_send, full_recv.at[half], in_plane(target))

    def start_parts(which):
        for chip in chips:
            other = seat_at(*chip)

            @pl.when((other < n_busy) & (2 * other + which != rank))
            def _():
                part_copy(2 * other + which).start()

    def start_line():
        for d in steps:
            line_copy(wrapped(line + d, n_line)).start()

    def start_full():
        for chip in chips:
            other = 2 * seat_at(*chip)
            for core in range(CORES):
                if chip == (0, 0):
                    continue
                full_copy(other + core).start()
        full_copy(2 * seat + 1 - half).start()

    def whole(ref, count, send, recv):
        part = ref.at[pl.ds(0, count)]
        return remote(part, part, send, recv, beside(1, 0))

    part_all = whole(gathered, n_plane - 1, part_send, part_recv)
    line_all = whole(column, n_line - 1, line_send, line_recv)

    def when_busy(busy_act, idle_act):
        pl.when(busy)(busy_act)
        if n_busy < n_seats:
            pl.when(jnp.logical_not(busy))(idle_act)

    def nothing():
        pass

    def wait_parts_sent():
        sent = 2 * n_busy
        when_busy(
            whole(gathered, sent - 1, part_send, part_recv).wait_send,
            whole(gathered, sent, part_send, part_recv).wait_send,
        )

    def wait_full(which):
        landed = n_busy * share
        mine = busy & (half == which)

        @pl.when(mine)
        def _():
            whole(total, landed - share, full_send, full_recv.at[which]).wait_recv()

        @pl.when(jnp.logical_not(mine))
        def _():
            whole(total, landed, full_send, full_recv.at[which]).wait_recv()

    def wait_full_sent():
        when_busy(
            whole(total, (n_plane - 1) * share, full_send, full_recv.at[0]).wait_send, nothing
        )

    def summed(ref, count):
        value = ref[0].astype(F32)
        for n in range(1, count):
            value = value + ref[n].astype(F32)
        return value

    copies_b = exchange(turned_b, cells_b, side_b, corner_b, halo_send_b, halo_recv_b)
    offsets = [(kx, ky, kz) for kx in (-1, 0, 1) for ky in (-1, 0, 1) for kz in (-1, 0, 1)]
    for which, own, field, sign in ((0, hidden, 1, -1), (1, delta, 0, 1)):
        sums = kernel_sums(own, cells_a, rim_a, field)
        parts = [sums[tuple(sign * o for o in offset)] for offset in offsets]
        parts.append(jnp.zeros((C, 128), F32))
        top = which * (PACKED // 2)
        for n, first in enumerate(range(0, 28, 4)):
            packed[pl.ds(top + n * C, C), :] = fold_four(*parts[first : first + 4])
        packed[pl.ds(top + 7 * C, C), :] = jnp.zeros((C, 128), F32)
        if which == 0:
            await_hail(0)
            hail(1)
        start_parts(which)


    await_hail(1)

    @pl.when(busy)
    def _():
        gathered[rank] = share_of(packed, rank)[...]
        part_all.wait_recv()
        column[line] = summed(gathered, n_plane).astype(BF16)
        start_line()

    place_rims(copies_b, cells_b, side_b, corner_b, rim_b)
    pre_two = conv_forward(cells_b, rim_b, band, rim_in, 1) * occupied
    middle = pl.ds(NZ, OWN)
    block_out = (cells_a[0, middle, :].astype(F32) + pre_two).astype(BF16)
    block_ref[...] = dot(reorder, block_out, ((1,), (1,))).astype(BF16)
    back = conv_backward(cells_b, rim_b, band, rim_out, 0) * occupied
    grad_features = (cells_a[1, middle, :].astype(F32) + back).astype(BF16)
    back_ref[...] = dot(reorder, grad_features, ((1,), (1,))).astype(BF16)

    @pl.when(busy)
    def _():
        line_all.wait_recv()
        share_of(total, rank)[...] = summed(column, n_line).astype(BF16)
        start_full()

    copies_a[1]()
    copies_b[1]()
    wait_parts_sent()
    pl.when(busy)(line_all.wait_send)
    groups = [(n, first, min(4, 27 - first)) for n, first in enumerate(range(0, 27, 4))]
    wait_full(0)
    for n, first, count in groups:
        group = total[pl.ds(n * C, C), :].astype(F32) * factor
        for k in range(count):
            two_ref[pl.ds((first + k) * C, C), :] = group[:, k * C : (k + 1) * C]
    wait_full(1)
    for n, first, count in groups:
        one_ref[pl.ds(first * C, count * C), :] = (
            total[pl.ds(PACKED // 2 + n * C, C), :].astype(F32).T[: count * C] * factor
        )
    wait_full_sent()


def deliver(*refs):
    results, outs, sems = refs[:4], refs[4:8], refs[8]
    copies = []
    for n, (result, out) in enumerate(zip(results, outs)):
        rows = result.shape[0] // PIECES
        for piece in range(PIECES):
            part = pl.ds(piece * rows, rows)
            sem = sems.at[n, piece]
            copies.append(pltpu.make_async_copy(result.at[part], out.at[part], sem))
    for copy in copies:
        copy.start()
    for copy in copies:
        copy.wait()


def per_device(features, brick_list, weight_one, weight_two, cotangent):
    n_gx, n_gy = lax.axis_size("gx"), lax.axis_size("gy")
    n_line, n_plane = n_gx // X_HI, X_HI * n_gy
    share = PACKED // n_plane
    factor = float(n_gx * SIDE * n_gy * SIDE * NZ) ** (-0.5)
    vmem = pl.BlockSpec(memory_space=pltpu.VMEM)
    halo = [
        pltpu.VMEM((2, LANES, OWN), BF16),
        pltpu.VMEM((2, ALL, LANES), BF16),
        pltpu.VMEM((2, 2, C, OWN), BF16),
        pltpu.VMEM((4, 2, C, 128), BF16),
        pltpu.VMEM((ALL, 128), BF16),
    ]
    out_shape = (
        jax.ShapeDtypeStruct((LANES, OWN), BF16),
        jax.ShapeDtypeStruct((LANES, OWN), BF16),
        jax.ShapeDtypeStruct((27 * C, C), F32),
        jax.ShapeDtypeStruct((27 * C, C), F32),
    )
    arguments = (
        brick_list,
        features.reshape(LANES, OWN),
        cotangent.reshape(LANES, OWN),
        weight_one.reshape(27 * C, C),
        weight_two.reshape(27 * C, C),
    )
    results = pl.pallas_call(
        functools.partial(kernel, n_gx, n_gy, factor),
        out_shape=tuple(pltpu.VMEM(result.shape, result.dtype) for result in out_shape),
        in_specs=[pl.BlockSpec(memory_space=pltpu.HBM)] * 5,
        out_specs=[vmem] * 4,
        scratch_shapes=halo
        + halo
        + [
            pltpu.VMEM((2, 27, C, 128), BF16),
            pltpu.VMEM((2, 3, LANES, 3 * LANES), BF16),
            pltpu.VMEM((2, 3, 128, 3 * LANES), BF16),
            pltpu.VMEM((2, 3, LANES, 3 * 128), BF16),
            pltpu.VMEM((PACKED, 128), F32),
            pltpu.VMEM((n_plane, share, 128), F32),
            pltpu.VMEM((n_line, share, 128), BF16),
            pltpu.VMEM((PACKED, 128), BF16),
        ]
        + [
            pltpu.SMEM((1, 1, BRICKS), jnp.int32),
            pltpu.VMEM((2, LANES, OWN), BF16),
            pltpu.VMEM((2, 27 * C, C), BF16),
        ]
        + [pltpu.SemaphoreType.DMA] * 5
        + [pltpu.SemaphoreType.DMA((3,))] * 4
        + [pltpu.SemaphoreType.DMA] * 5
        + [pltpu.SemaphoreType.DMA((2,))]
        + [pltpu.SemaphoreType.REGULAR((2,))],
        compiler_params=pltpu.CompilerParams(
            collective_id=0, has_side_effects=True, vmem_limit_bytes=40 * 1024 * 1024
        ),
    )(*[pltpu.with_memory_space_constraint(value, pltpu.HBM) for value in arguments])
    block_out, grad_features, one, two = pl.pallas_call(
        deliver,
        out_shape=out_shape,
        in_specs=[vmem] * 4,
        out_specs=[pl.BlockSpec(memory_space=pl.ANY)] * 4,
        scratch_shapes=[pltpu.SemaphoreType.DMA((4, PIECES))],
        compiler_params=pltpu.CompilerParams(vmem_limit_bytes=4 * 1024 * 1024),
    )(*[pltpu.with_memory_space_constraint(value, pltpu.VMEM) for value in results])
    flat = (C, SIDE, OWN)
    cube = (3, 3, 3, C, C)
    return block_out.reshape(flat), grad_features.reshape(flat), one.reshape(cube), two.reshape(cube)


def solution(mesh):
    return jax.shard_map(
        per_device,
        mesh=mesh,
        in_specs=(P(None, "gx", "gy"), P("gx", "gy", None), P(), P(), P(None, "gx", "gy")),
        out_specs=(P(None, "gx", "gy"), P(None, "gx", "gy"), P(), P()),
        check_vma=False,
    )
```

```python
import functools

import jax
import jax.numpy as jnp
from jax import lax
from jax.experimental import pallas as pl
from jax.experimental.pallas import tpu as pltpu
from jax.sharding import PartitionSpec as P

C = 32
SIDE = 8
NZ = 48
BRICKS = 6
LANES = SIDE * C
OWN = SIDE * NZ
ALL = OWN + 2 * NZ
PACKED = 512
PIECES = 4
X_HI = 2
REACH = 3
X_LO = 2
CORES = 2
MESH = pl.DeviceIdType.MESH
F32 = jnp.float32
BF16 = jnp.bfloat16


def dot(a, b, contract=((1,), (0,))):
    return lax.dot_general(a, b, (contract, ((), ())), preferred_element_type=F32)


def rows_mask(zero_at):
    z = lax.broadcasted_iota(jnp.int32, (NZ, LANES), 0)
    return jnp.concatenate([jnp.where(z == zero_at, 0.0, 1.0).astype(F32)] * SIDE, axis=0)


def from_below(value):
    return pltpu.roll(value, 1, 0) * rows_mask(0)


def from_above(value):
    return pltpu.roll(value, OWN - 1, 0) * rows_mask(NZ - 1)


def at(kx, ky, kz):
    return kx * 9 + ky * 3 + kz


def lane_block(shape=(C, 128)):
    return lax.broadcasted_iota(jnp.int32, shape, 1) // C


def widen_weights(w_ref, quad, which):
    lane = lax.broadcasted_iota(jnp.int32, (C, 128), 1)
    row = lax.broadcasted_iota(jnp.int32, (C, 128), 0)
    repeat = jnp.where(lane % C == row, 1.0, 0.0).astype(BF16)
    quad[which] = dot(w_ref[which], repeat).astype(BF16).reshape(27, C, 128)


def build_bands(quad, band, rim_in, rim_out):
    blocks = lane_block()
    masks = [jnp.where(blocks == b, 1.0, 0.0).astype(BF16) for b in range(4)]
    zero = jnp.zeros((C, 128), BF16)

    def step(i, carry):
        w, ky = i // 3, lax.rem(i, 3)
        rim_in[w, ky] = jnp.zeros((128, 3 * LANES), BF16)
        rim_out[w, ky] = jnp.zeros((LANES, 3 * 128), BF16)
        for kz in range(3):
            parts = [quad[w, at(kx, ky, kz)] for kx in range(3)]
            for xi in range(SIDE):
                for tile in range(2):
                    value = None
                    for kx in range(3):
                        xo = xi + 1 - kx - 4 * tile
                        if 0 <= xo < 4:
                            term = parts[kx] * masks[xo]
                            value = term if value is None else value + term
                    lanes = pl.ds(kz * LANES + tile * 128, 128)
                    band[w, ky, pl.ds(xi * C, C), lanes] = zero if value is None else value
            rim_in[w, ky, pl.ds(0, C), pl.ds(kz * LANES, 128)] = parts[0] * masks[0]
            rim_in[w, ky, pl.ds(C, C), pl.ds(kz * LANES + 128, 128)] = parts[2] * masks[3]
            rim_out[w, ky, pl.ds(0, C), pl.ds(kz * 128, 128)] = parts[2] * masks[2]
            rim_out[w, ky, pl.ds(LANES - C, C), pl.ds(kz * 128, 128)] = parts[0] * masks[3]
        return carry

    lax.fori_loop(0, 6, step, 0)


def shifted_rows(cells, rim, field):
    parts = [cells[field, pl.ds(ky * NZ, OWN), :] for ky in range(3)]
    return jnp.concatenate(parts + [rim[pl.ds(ky * NZ, OWN), :] for ky in range(3)], axis=1)


def conv_forward(cells, rim, band, rim_in, w):
    lhs = shifted_rows(cells, rim, 0)
    terms = []
    for kz in range(3):
        lanes = pl.ds(kz * LANES, LANES)
        rhs = jnp.concatenate(
            [band[w, ky, :, lanes] for ky in range(3)]
            + [rim_in[w, ky, :, lanes] for ky in range(3)],
            axis=0,
        )
        terms.append(dot(lhs, rhs))
    return terms[1] + from_below(terms[0]) + from_above(terms[2])


def conv_backward(cells, rim, band, rim_out, w):
    lhs = shifted_rows(cells, rim, 1)
    terms = []
    for kz in range(3):
        back = 2 - kz
        rhs = jnp.concatenate(
            [band[w, 2 - ky, :, pl.ds(back * LANES, LANES)] for ky in range(3)]
            + [rim_out[w, 2 - ky, :, pl.ds(back * 128, 128)] for ky in range(3)],
            axis=1,
        )
        terms.append(dot(lhs, rhs, ((1,), (1,))))
    return terms[1] + from_below(terms[0]) + from_above(terms[2])


def kernel_sums(own, cells, rim, field):
    wide = own.astype(F32)
    turned = {
        -1: from_above(wide).astype(BF16).T,
        0: own.T,
        1: from_below(wide).astype(BF16).T,
    }
    tall = jnp.concatenate([turned[sz] for sz in (-1, 0, 1)], axis=0)
    ends = jnp.concatenate(
        [turned[sz][part] for sz in (-1, 0, 1) for part in (slice(0, C), slice(LANES - C, LANES))],
        axis=0,
    )
    blocks = lane_block()
    sums = {}
    shifts = [pl.ds(shift * NZ, OWN) for shift in range(3)]
    mains = dot(tall, jnp.concatenate([cells[field, rows, :] for rows in shifts], axis=1))
    edges = dot(ends, jnp.concatenate([rim[rows, :] for rows in shifts], axis=1))
    for sy in (-1, 0, 1):
        main = mains[:, (1 + sy) * LANES : (2 + sy) * LANES]
        edge = edges[:, (1 + sy) * 128 : (2 + sy) * 128]
        for n, sz in enumerate((-1, 0, 1)):
            for sx in (-1, 0, 1):
                halves = []
                for tile in range(2):
                    value = None
                    for b in range(4):
                        a = 4 * tile + b - sx
                        if 0 <= a < SIDE:
                            top = n * LANES + a * C
                            term = main[top : top + C, tile * 128 : tile * 128 + 128]
                        else:
                            term = jnp.zeros((C, 128), F32)
                        value = term if value is None else jnp.where(blocks >= b, term, value)
                    halves.append(value)
                total = halves[0] + halves[1]
                if sx == -1:
                    total = total + jnp.where(blocks == 2 * field, edge[n * 64 : n * 64 + C], 0.0)
                if sx == 1:
                    total = total + jnp.where(
                        blocks == 2 * field + 1, edge[n * 64 + C : n * 64 + 64], 0.0
                    )
                sums[sx, sy, sz] = total
    return sums


def fold_four(a, b, c, d):
    blocks = lane_block()
    low = blocks < 2
    middle = (blocks == 1) | (blocks == 2)
    even = (blocks == 0) | (blocks == 2)
    ac = jnp.where(low, a, c) + pltpu.roll(jnp.where(low, c, a), 64, 1)
    bd = jnp.where(middle, b, d) + pltpu.roll(jnp.where(middle, d, b), 64, 1)
    return jnp.where(even, ac, bd) + pltpu.roll(jnp.where(even, bd, ac), 96, 1)


def kernel(
    n_gx, n_gy, factor,
    list_any, f_any, g_any, w1_any, w2_any,
    block_ref, back_ref, one_ref, two_ref,
    turned_a, cells_a, side_a, corner_a, rim_a,
    turned_b, cells_b, side_b, corner_b, rim_b,
    quad, band, rim_in, rim_out,
    packed, gathered, column, total,
    list_ref, fields_in, weights_in,
    list_sem, f_sem, g_sem, w1_sem, w2_sem,
    halo_send_a, halo_recv_a, halo_send_b, halo_recv_b,
    part_send, part_recv, line_send, line_recv, full_send, full_recv, hails,
):
    gx, gy = lax.axis_index("gx"), lax.axis_index("gy")
    n_line = n_gx // X_HI
    n_plane = X_HI * n_gy
    x_hi = jnp.where(gx >= n_line, 1, 0)
    line = gx - x_hi * n_line
    rank = x_hi * n_gy + gy
    share = PACKED // n_plane
    n_seats = n_plane // 2
    n_busy = -(-7 * C // share)
    seat = rank // 2
    half = rank - 2 * seat
    busy = seat < n_busy

    def wrapped(value, count):
        value = jnp.where(value >= count, value - count, value)
        return jnp.where(value < 0, value + count, value)

    def beside(dx, dy):
        return (wrapped(gx + dx, n_gx), wrapped(gy + dy, n_gy))

    def in_plane(other):
        hi = jnp.where(other >= n_gy, 1, 0)
        return (hi * n_line + line, other - hi * n_gy)

    def in_line(other):
        return (x_hi * n_line + other, gy)

    n_x, n_y = X_HI * X_LO, n_gy // (X_LO * CORES)
    y = gy // (X_LO * CORES)
    x = x_hi * X_LO + gy // CORES - y * X_LO

    def hops(offset, count):
        return min(offset, count - offset)

    chips = [(dy, dx) for dy in range(n_y) for dx in range(n_x)]
    chips.sort(key=lambda chip: -hops(chip[0], n_y) - hops(chip[1], n_x))
    steps = sorted(range(1, n_line), key=lambda d: -hops(d, n_line))

    def seat_at(dy, dx):
        other_y, other_x = wrapped(y + dy, n_y), wrapped(x + dx, n_x)
        hi = jnp.where(other_x >= X_LO, 1, 0)
        return hi * (n_seats - n_seats // X_HI) + other_y * X_LO + other_x - hi * X_LO

    barrier = pltpu.get_barrier_semaphore()
    around = [(dx, dy) for dx in (-1, 0, 1) for dy in (-1, 0, 1) if (dx, dy) != (0, 0)]
    far_chips = [chip for chip in chips if hops(chip[0], n_y) + hops(chip[1], n_x) > REACH]
    far_line = [d for d in steps if hops(d, n_line) > REACH]
    around.sort(key=lambda step: -abs(step[0]) - abs(step[1]))
    greeted = [beside(dx, dy) for dx, dy in around]
    greeted += [in_line(wrapped(line + d, n_line)) for d in steps if d not in far_line]
    for chip in chips:
        if chip not in far_chips and chip != (0, 0):
            greeted += [in_plane(2 * seat_at(*chip) + core) for core in range(CORES)]
    greeted.append(in_plane(2 * seat + 1 - half))
    for target in greeted:
        pl.semaphore_signal(barrier, inc=1, device_id=target, device_id_type=MESH)

    hailed = [[], []]
    if far_chips:
        hailed[0].append(in_plane(2 * seat_at(n_y - 1, 0) + half))
    if far_line:
        hailed[0] += [in_line(wrapped(line + d, n_line)) for d in (REACH, -REACH)]
        rest = n_line // 2 - 2 * REACH
        hailed[1] += [in_line(wrapped(line + d, n_line)) for d in (rest, -rest)]

    def hail(n):
        for target in hailed[n]:
            pl.semaphore_signal(hails.at[n], inc=1, device_id=target, device_id_type=MESH)

    def await_hail(n):
        if hailed[n]:
            pl.semaphore_wait(hails.at[n], len(hailed[n]))

    loads = [
        pltpu.make_async_copy(src, dst, sem)
        for src, dst, sem in (
            (list_any, list_ref, list_sem),
            (f_any, fields_in.at[0], f_sem),
            (g_any, fields_in.at[1], g_sem),
            (w1_any, weights_in.at[0], w1_sem),
            (w2_any, weights_in.at[1], w2_sem),
        )
    ]
    for load in loads:
        load.start()

    loads[0].wait()
    hits = []
    for brick in range(BRICKS):
        count = jnp.int32(0)
        for slot in range(BRICKS):
            count = count + jnp.where(list_ref[0, 0, slot] == brick, 1, 0)
        hits.append(count.astype(F32))
    occupied = jnp.concatenate(
        [jnp.full((8, LANES), hit, F32) for hit in hits] * SIDE, axis=0
    )
    brick_of = lax.rem(lax.broadcasted_iota(jnp.int32, (8, OWN), 1), NZ) // 8
    across = jnp.zeros((8, OWN), F32)
    for brick in range(BRICKS):
        across = across + jnp.where(brick_of == brick, hits[brick], 0.0)
    across = jnp.concatenate([across] * (LANES // 8), axis=0)

    row = lax.broadcasted_iota(jnp.int32, (LANES, LANES), 0)
    col = lax.broadcasted_iota(jnp.int32, (LANES, LANES), 1)
    order = jnp.where(col == (row % C) * SIDE + row // C, 1.0, 0.0).astype(BF16)
    reorder = jnp.where(row == (col % C) * SIDE + col // C, 1.0, 0.0).astype(BF16)
    for field in range(2):
        loads[1 + field].wait()
        value = (dot(order, fields_in[field]) * across).astype(BF16)
        turned_a[field] = value
        cells_a[field, pl.ds(NZ, OWN), :] = value.T

    pl.semaphore_wait(barrier, len(greeted))

    def exchange(turned, cells, side, corner, send, recv):
        low, high = pl.ds(0, C), pl.ds(LANES - C, C)
        every, head, tail = pl.ds(0, OWN), pl.ds(0, 128), pl.ds(OWN - 128, 128)

        def strip(rows, lanes):
            return turned.at[:, rows, lanes]

        def slab(y):
            return cells.at[:, pl.ds((y + 1) * NZ, NZ), :]

        def remote_copy(src, dst, group, dx, dy):
            return pltpu.make_async_remote_copy(
                src_ref=src,
                dst_ref=dst,
                send_sem=send.at[group],
                recv_sem=recv.at[group],
                device_id=beside(dx, dy),
                device_id_type=MESH,
            )

        @pl.when(gx < n_gx - 1)
        def _():
            remote_copy(strip(high, tail), corner.at[0], 1, 1, 1).start()
            remote_copy(strip(high, head), corner.at[2], 1, 1, -1).start()
            remote_copy(strip(high, every), side.at[0], 1, 1, 0).start()

        @pl.when(gx > 0)
        def _():
            remote_copy(strip(low, tail), corner.at[1], 2, -1, 1).start()
            remote_copy(strip(low, head), corner.at[3], 2, -1, -1).start()
            remote_copy(strip(low, every), side.at[1], 2, -1, 0).start()

        remote_copy(slab(SIDE - 1), slab(-1), 0, 0, 1).start()
        remote_copy(slab(0), slab(SIDE), 0, 0, -1).start()

        slabs = turned.at[0, pl.ds(0, 2 * NZ * 2), pl.ds(0, 256)]
        strips = turned.at[0, pl.ds(0, 160), pl.ds(0, 256)]

        def wait_recv():
            remote_copy(slabs, slabs, 0, 0, 1).wait_recv()

            @pl.when(gx > 0)
            def _():
                remote_copy(strips, strips, 1, 1, 0).wait_recv()

            @pl.when(gx < n_gx - 1)
            def _():
                remote_copy(strips, strips, 2, 1, 0).wait_recv()

        def wait_send():
            remote_copy(slabs, slabs, 0, 0, 1).wait_send()

            @pl.when(gx < n_gx - 1)
            def _():
                remote_copy(strips, strips, 1, 1, 0).wait_send()

            @pl.when(gx > 0)
            def _():
                remote_copy(strips, strips, 2, 1, 0).wait_send()

        return wait_recv, wait_send

    def place_rims(copies, cells, side, corner, rim):
        copies[0]()
        first_y, last_y = gy > 0, gy < n_gy - 1
        for rows, keep in ((pl.ds(0, NZ), first_y), (pl.ds(ALL - NZ, NZ), last_y)):
            for field in range(2):
                kept = jnp.where(keep, cells[field, rows, :].astype(F32), 0.0)
                cells[field, rows, :] = kept.astype(BF16)
        odd = lax.rem(lane_block((1, 128)), 2)
        inside = jnp.where(odd == 1, jnp.where(gx < n_gx - 1, 1, 0), jnp.where(gx > 0, 1, 0))

        def turn(left, right, keep):
            parts = [left[0], right[0], left[1], right[1]]
            value = jnp.concatenate(parts, axis=0).T.astype(F32)
            return jnp.where(inside * jnp.where(keep, 1, 0) > 0, value, 0.0).astype(BF16)

        rim[pl.ds(NZ, OWN), :] = turn(side[0], side[1], True)
        rim[pl.ds(0, NZ), :] = turn(corner[0], corner[1], first_y)[128 - NZ :]
        rim[pl.ds(ALL - NZ, NZ), :] = turn(corner[2], corner[3], last_y)[:NZ]

    copies_a = exchange(turned_a, cells_a, side_a, corner_a, halo_send_a, halo_recv_a)
    hail(0)
    for w in range(2):
        loads[3 + w].wait()
        widen_weights(weights_in, quad, w)
    build_bands(quad, band, rim_in, rim_out)
    place_rims(copies_a, cells_a, side_a, corner_a, rim_a)

    pre_one = conv_forward(cells_a, rim_a, band, rim_in, 0) * occupied
    sigma = jax.nn.sigmoid(pre_one)
    hidden = (pre_one * sigma).astype(BF16)
    slope = occupied * sigma * (1.0 + pre_one * (1.0 - sigma))
    delta = (conv_backward(cells_a, rim_a, band, rim_out, 1) * slope).astype(BF16)
    for field, value in enumerate((hidden, delta)):
        cells_b[field, pl.ds(NZ, OWN), :] = value
        turned_b[field] = value.T

    def share_of(ref, other):
        other_seat = other // 2
        top = (other - 2 * other_seat) * (PACKED // 2) + other_seat * share
        return ref.at[pl.ds(pl.multiple_of(top, share), share), :]

    def remote(src, dst, send, recv, device):
        return pltpu.make_async_remote_copy(
            src_ref=src,
            dst_ref=dst,
            send_sem=send,
            recv_sem=recv,
            device_id=device,
            device_id_type=MESH,
        )

    def part_copy(target):
        src, dst = share_of(packed, target), gathered.at[rank]
        return remote(src, dst, part_send, part_recv, in_plane(target))

    def line_copy(target):
        src, dst = column.at[line], column.at[line]
        return remote(src, dst, line_send, line_recv, in_line(target))

    def full_copy(target):
        src, dst = share_of(total, rank), share_of(total, rank)
        return remote(src, dst, full_send, full_recv.at[half], in_plane(target))

    def start_parts(which):
        for chip in chips:
            other = seat_at(*chip)

            @pl.when((other < n_busy) & (2 * other + which != rank))
            def _():
                part_copy(2 * other + which).start()

    def start_line():
        for d in steps:
            line_copy(wrapped(line + d, n_line)).start()

    def start_full():
        for chip in chips:
            other = 2 * seat_at(*chip)
            for core in range(CORES):
                if chip == (0, 0):
                    continue
                full_copy(other + core).start()
        full_copy(2 * seat + 1 - half).start()

    def whole(ref, count, send, recv):
        part = ref.at[pl.ds(0, count)]
        return remote(part, part, send, recv, beside(1, 0))

    part_all = whole(gathered, n_plane - 1, part_send, part_recv)
    line_all = whole(column, n_line - 1, line_send, line_recv)

    def when_busy(busy_act, idle_act):
        pl.when(busy)(busy_act)
        if n_busy < n_seats:
            pl.when(jnp.logical_not(busy))(idle_act)

    def nothing():
        pass

    def wait_parts_sent():
        sent = 2 * n_busy
        when_busy(
            whole(gathered, sent - 1, part_send, part_recv).wait_send,
            whole(gathered, sent, part_send, part_recv).wait_send,
        )

    def wait_full(which):
        landed = n_busy * share
        mine = busy & (half == which)

        @pl.when(mine)
        def _():
            whole(total, landed - share, full_send, full_recv.at[which]).wait_recv()

        @pl.when(jnp.logical_not(mine))
        def _():
            whole(total, landed, full_send, full_recv.at[which]).wait_recv()

    def wait_full_sent():
        when_busy(
            whole(total, (n_plane - 1) * share, full_send, full_recv.at[0]).wait_send, nothing
        )

    def summed(ref, count):
        value = ref[0].astype(F32)
        for n in range(1, count):
            value = value + ref[n].astype(F32)
        return value

    copies_b = exchange(turned_b, cells_b, side_b, corner_b, halo_send_b, halo_recv_b)
    offsets = [(kx, ky, kz) for kx in (-1, 0, 1) for ky in (-1, 0, 1) for kz in (-1, 0, 1)]
    for which, own, field, sign in ((0, hidden, 1, -1), (1, delta, 0, 1)):
        sums = kernel_sums(own, cells_a, rim_a, field)
        parts = [sums[tuple(sign * o for o in offset)] for offset in offsets]
        parts.append(jnp.zeros((C, 128), F32))
        top = which * (PACKED // 2)
        for n, first in enumerate(range(0, 28, 4)):
            packed[pl.ds(top + n * C, C), :] = fold_four(*parts[first : first + 4])
        packed[pl.ds(top + 7 * C, C), :] = jnp.zeros((C, 128), F32)
        if which == 0:
            await_hail(0)
            hail(1)
        start_parts(which)


    await_hail(1)

    @pl.when(busy)
    def _():
        gathered[rank] = share_of(packed, rank)[...]
        part_all.wait_recv()
        column[line] = summed(gathered, n_plane).astype(BF16)
        start_line()

    place_rims(copies_b, cells_b, side_b, corner_b, rim_b)
    pre_two = conv_forward(cells_b, rim_b, band, rim_in, 1) * occupied
    middle = pl.ds(NZ, OWN)
    block_out = (cells_a[0, middle, :].astype(F32) + pre_two).astype(BF16)
    block_ref[...] = dot(reorder, block_out, ((1,), (1,))).astype(BF16)
    back = conv_backward(cells_b, rim_b, band, rim_out, 0) * occupied
    grad_features = (cells_a[1, middle, :].astype(F32) + back).astype(BF16)
    back_ref[...] = dot(reorder, grad_features, ((1,), (1,))).astype(BF16)

    @pl.when(busy)
    def _():
        line_all.wait_recv()
        share_of(total, rank)[...] = summed(column, n_line).astype(BF16)
        start_full()

    copies_a[1]()
    copies_b[1]()
    wait_parts_sent()
    pl.when(busy)(line_all.wait_send)
    groups = [(n, first, min(4, 27 - first)) for n, first in enumerate(range(0, 27, 4))]
    wait_full(0)
    for n, first, count in groups:
        group = total[pl.ds(n * C, C), :].astype(F32) * factor
        for k in range(count):
            two_ref[pl.ds((first + k) * C, C), :] = group[:, k * C : (k + 1) * C]
    wait_full(1)
    for n, first, count in groups:
        one_ref[pl.ds(first * C, count * C), :] = (
            total[pl.ds(PACKED // 2 + n * C, C), :].astype(F32).T[: count * C] * factor
        )
    wait_full_sent()


def deliver(*refs):
    results, outs, sems = refs[:4], refs[4:8], refs[8]
    copies = []
    for n, (result, out) in enumerate(zip(results, outs)):
        rows = result.shape[0] // PIECES
        for piece in range(PIECES):
            part = pl.ds(piece * rows, rows)
            sem = sems.at[n, piece]
            copies.append(pltpu.make_async_copy(result.at[part], out.at[part], sem))
    for copy in copies:
        copy.start()
    for copy in copies:
        copy.wait()


def per_device(features, brick_list, weight_one, weight_two, cotangent):
    n_gx, n_gy = lax.axis_size("gx"), lax.axis_size("gy")
    n_line, n_plane = n_gx // X_HI, X_HI * n_gy
    share = PACKED // n_plane
    factor = float(n_gx * SIDE * n_gy * SIDE * NZ) ** (-0.5)
    vmem = pl.BlockSpec(memory_space=pltpu.VMEM)
    halo = [
        pltpu.VMEM((2, LANES, OWN), BF16),
        pltpu.VMEM((2, ALL, LANES), BF16),
        pltpu.VMEM((2, 2, C, OWN), BF16),
        pltpu.VMEM((4, 2, C, 128), BF16),
        pltpu.VMEM((ALL, 128), BF16),
    ]
    out_shape = (
        jax.ShapeDtypeStruct((LANES, OWN), BF16),
        jax.ShapeDtypeStruct((LANES, OWN), BF16),
        jax.ShapeDtypeStruct((27 * C, C), F32),
        jax.ShapeDtypeStruct((27 * C, C), F32),
    )
    arguments = (
        brick_list,
        features.reshape(LANES, OWN),
        cotangent.reshape(LANES, OWN),
        weight_one.reshape(27 * C, C),
        weight_two.reshape(27 * C, C),
    )
    results = pl.pallas_call(
        functools.partial(kernel, n_gx, n_gy, factor),
        out_shape=tuple(pltpu.VMEM(result.shape, result.dtype) for result in out_shape),
        in_specs=[pl.BlockSpec(memory_space=pltpu.HBM)] * 5,
        out_specs=[vmem] * 4,
        scratch_shapes=halo
        + halo
        + [
            pltpu.VMEM((2, 27, C, 128), BF16),
            pltpu.VMEM((2, 3, LANES, 3 * LANES), BF16),
            pltpu.VMEM((2, 3, 128, 3 * LANES), BF16),
            pltpu.VMEM((2, 3, LANES, 3 * 128), BF16),
            pltpu.VMEM((PACKED, 128), F32),
            pltpu.VMEM((n_plane, share, 128), F32),
            pltpu.VMEM((n_line, share, 128), BF16),
            pltpu.VMEM((PACKED, 128), BF16),
        ]
        + [
            pltpu.SMEM((1, 1, BRICKS), jnp.int32),
            pltpu.VMEM((2, LANES, OWN), BF16),
            pltpu.VMEM((2, 27 * C, C), BF16),
        ]
        + [pltpu.SemaphoreType.DMA] * 5
        + [pltpu.SemaphoreType.DMA((3,))] * 4
        + [pltpu.SemaphoreType.DMA] * 5
        + [pltpu.SemaphoreType.DMA((2,))]
        + [pltpu.SemaphoreType.REGULAR((2,))],
        compiler_params=pltpu.CompilerParams(
            collective_id=0, has_side_effects=True, vmem_limit_bytes=40 * 1024 * 1024
        ),
    )(*[pltpu.with_memory_space_constraint(value, pltpu.HBM) for value in arguments])
    block_out, grad_features, one, two = pl.pallas_call(
        deliver,
        out_shape=out_shape,
        in_specs=[vmem] * 4,
        out_specs=[pl.BlockSpec(memory_space=pl.ANY)] * 4,
        scratch_shapes=[pltpu.SemaphoreType.DMA((4, PIECES))],
        compiler_params=pltpu.CompilerParams(vmem_limit_bytes=4 * 1024 * 1024),
    )(*[pltpu.with_memory_space_constraint(value, pltpu.VMEM) for value in results])
    flat = (C, SIDE, OWN)
    cube = (3, 3, 3, C, C)
    return block_out.reshape(flat), grad_features.reshape(flat), one.reshape(cube), two.reshape(cube)


def solution(mesh):
    return jax.shard_map(
        per_device,
        mesh=mesh,
        in_specs=(P(None, "gx", "gy"), P("gx", "gy", None), P(), P(), P(None, "gx", "gy")),
        out_specs=(P(None, "gx", "gy"), P(None, "gx", "gy"), P(), P()),
        check_vma=False,
    )
```
